32 devices in a mesh: fsdp: 2 (over y), ctx: 4 (over x, core), tensor: 4 (over z).
Axes of the slice: x: 2, y: 2, z: 4, core: 2. Of those that a mesh axis runs over, the one named last changes fastest.
Arguments:
- latents_in: bfloat16 [6, 1024, 768], P('fsdp', 'ctx'), may hold values from -6 to 6
- conditioning: bfloat16 [6, 768], P('fsdp'), may hold values from -6 to 6
- ada_weight: bfloat16 [768, 6, 768], P(('fsdp', 'ctx'), None, 'tensor'), may hold values from -0.21875 to 0.21875
- ada_bias: bfloat16 [6, 768], P(None, ('tensor', 'fsdp', 'ctx')), may hold values from -3 to 3
- qkv_weight: bfloat16 [768, 3, 768], P(('fsdp', 'ctx'), None, 'tensor'), may hold values from -0.21875 to 0.21875
- qv_bias: bfloat16 [2, 768], P(None, ('tensor', 'fsdp', 'ctx')), may hold values from -3 to 3
- out_weight: bfloat16 [768, 768], P('tensor', ('fsdp', 'ctx')), may hold values from -1.75 to 1.75
- out_bias: bfloat16 [768], P(('fsdp', 'ctx')), may hold values from -3 to 3
- up_weight: bfloat16 [768, 3072], P(('fsdp', 'ctx'), 'tensor'), may hold values from -0.21875 to 0.21875
- up_bias: bfloat16 [3072], P(('tensor', 'fsdp', 'ctx')), may hold values from -3 to 3
- down_weight: bfloat16 [3072, 768], P('tensor', ('fsdp', 'ctx')), may hold values from -0.109375 to 0.109375
- down_bias: bfloat16 [768], P(('fsdp', 'ctx')), may hold values from -3 to 3
- cotangent: bfloat16 [6, 1024, 768], P('fsdp', 'ctx'), may hold values from -6 to 6
Outputs:
- block_out: bfloat16 [6, 1024, 768], P('fsdp', 'ctx')
- grad_in: float32 [6, 1024, 768], P('fsdp', 'ctx')
- grad_cond: float32 [6, 768], P('fsdp')
- grad_ada_weight: float32 [768, 6, 768], P(('fsdp', 'ctx'), None, 'tensor')
- grad_ada_bias: float32 [6, 768], P(None, ('tensor', 'fsdp', 'ctx'))
- grad_qkv_weight: float32 [768, 3, 768], P(('fsdp', 'ctx'), None, 'tensor')
- grad_qv_bias: float32 [2, 768], P(None, ('tensor', 'fsdp', 'ctx'))
- grad_out_weight: float32 [768, 768], P('tensor', ('fsdp', 'ctx'))
- grad_out_bias: float32 [768], P(('fsdp', 'ctx'))
- grad_up_weight: float32 [768, 3072], P(('fsdp', 'ctx'), 'tensor')
- grad_up_bias: float32 [3072], P(('tensor', 'fsdp', 'ctx'))
- grad_down_weight: float32 [3072, 768], P('tensor', ('fsdp', 'ctx'))
- grad_down_bias: float32 [768], P(('fsdp', 'ctx'))
The draws below stay inside these ranges and needn't reach their ends.
All inputs are finite; a program needn't handle non-finite values.
Results may differ from the reference program's by a relative error of at most 0.017.
Values may be sent and summed in bfloat16 or wider, within the bound.
A program may use at most 128 MiB of HBM per device.

```python
import math
import jax
import jax.numpy as jnp
from jax import lax

D = 768
HEAD_DIM = 64
FF = 3072
SEQ = 1024
LATENTS = 6


def levels(stream_key, dims, shards, smallest, top_value):
    loudness = 1.0
    for dim, parts in shards:
        steps = jax.random.uniform(jax.random.fold_in(jax.random.fold_in(stream_key, 6), dim), (parts,), jnp.float32, smallest / len(shards), top_value / len(shards))
        loudness = loudness * jnp.repeat(jnp.exp(steps), dims[dim] // parts).reshape((-1,) + (1,) * (len(dims) - 1 - dim))
    return loudness


def scatter_about(rng, extent, deviation, limit, pieces=(), kind=jnp.bfloat16):
    drawn = jax.random.normal(rng, extent, jnp.float32) * deviation
    if len(pieces) > 0:
        drawn = levels(rng, extent, pieces, -0.22, 0.18) * drawn
    return jnp.clip(drawn, min=-limit, max=limit).astype(kind)


def setup_inputs(seed: int = 0) -> dict:
    key_list = jax.random.split(jax.random.key(seed), 14)
    latents_in = scatter_about(key_list[0], (LATENTS, SEQ, D), 1.0, 6.0, ((0, 2), (1, 4)))
    conditioning = scatter_about(key_list[1], (LATENTS, D), 1.0, 6.0, ((0, 2),))
    ada_weight = scatter_about(key_list[2], (D, 6, D), D ** -0.5, 0.21875, ((0, 8), (2, 4)))
    ada_bias = scatter_about(key_list[3], (6, D), 0.5, 3.0, ((1, 32),))
    qkv_weight = scatter_about(key_list[4], (D, 3, D), D ** -0.5, 0.21875, ((0, 8), (2, 4)))
    qv_bias = scatter_about(key_list[5], (2, D), 0.5, 3.0, ((1, 32),))
    out_weight = scatter_about(key_list[6], (D, D), (D // 64) ** -0.5, 1.75, ((0, 4), (1, 8)))
    out_bias = scatter_about(key_list[7], (D,), 0.5, 3.0, ((0, 8),))
    up_weight = scatter_about(key_list[8], (D, FF), D ** -0.5, 0.21875, ((0, 8), (1, 4)))
    up_bias = scatter_about(key_list[9], (FF,), 0.5, 3.0, ((0, 32),))
    down_weight = scatter_about(key_list[10], (FF, D), FF ** -0.5, 0.109375, ((0, 4), (1, 8)))
    down_bias = scatter_about(key_list[11], (D,), 0.5, 3.0, ((0, 8),))
    cotangent = scatter_about(key_list[12], (LATENTS, SEQ, D), 1.0, 6.0, ((0, 2), (1, 4)))
    return {"latents_in": latents_in, "conditioning": conditioning, "ada_weight": ada_weight, "ada_bias": ada_bias, "qkv_weight": qkv_weight, "qv_bias": qv_bias, "out_weight": out_weight, "out_bias": out_bias, "up_weight": up_weight, "up_bias": up_bias, "down_weight": down_weight, "down_bias": down_bias, "cotangent": cotangent}


EPSILON = 1e-06
GELU_SCALE = 0.7978845608028654
GELU_CUBIC = 0.044715

@jax.custom_vjp
def low(v):
    return lax.optimization_barrier(v.astype(jnp.bfloat16)).astype(jnp.float32)

@jax.custom_vjp
def low_back(v):
    return v

def low_keep(v):
    return (low(v), None)

def low_pass(kept, grad):
    return (grad,)

def back_keep(v):
    return (v, None)

def back_low(kept, grad):
    return (low(grad),)
low.defvjp(low_keep, low_pass)
low_back.defvjp(back_keep, back_low)

def precise(form, left, right):
    return jnp.einsum(form, left, right, precision=lax.Precision.HIGHEST)

def layer_norm(values):
    center = values - lax.optimization_barrier(jnp.mean(values, axis=-1, keepdims=True))
    spread = lax.optimization_barrier(jnp.mean(center * center, axis=-1, keepdims=True))
    return center * lax.rsqrt(spread + EPSILON)

def gelu_tanh(pre_act):
    return 0.5 * pre_act * (1.0 + jnp.tanh(GELU_SCALE * (pre_act + GELU_CUBIC * pre_act * pre_act * pre_act)))

def one_latent(tokens, modulation, weights):
    qkv_weight, qv_bias, out_weight, out_bias, up_weight, up_bias, down_weight, down_bias = weights
    length = tokens.shape[0]
    feature_width = tokens.shape[1]
    head_count = feature_width // HEAD_DIM
    score_scale = 1.0 / math.sqrt(HEAD_DIM)
    normed = layer_norm(tokens)
    shifted = low(normed * (1.0 + modulation[1]) + modulation[0])
    project = precise('sd,dje->sje', shifted, qkv_weight)
    queries = low_back(low(project[:, 0] + qv_bias[0]))
    key_rows = low_back(low(project[:, 1]))
    value_rows = low_back(low(project[:, 2] + qv_bias[1]))
    query_heads = queries.reshape(length, head_count, HEAD_DIM)
    key_heads = key_rows.reshape(length, head_count, HEAD_DIM)
    value_heads = value_rows.reshape(length, head_count, HEAD_DIM)
    scores = low_back(precise('qhe,khe->hqk', query_heads, key_heads) * score_scale)
    prob_low = low(jax.nn.softmax(scores, axis=-1))
    mixed_heads = precise('hqk,khe->qhe', prob_low, value_heads).reshape(length, feature_width)
    mixed_heads = low_back(low(mixed_heads))
    attended = low_back(precise('sd,de->se', mixed_heads, out_weight) + out_bias)
    after_attn = tokens + modulation[2] * attended
    normed_two = layer_norm(after_attn)
    shifted_two = low(normed_two * (1.0 + modulation[4]) + modulation[3])
    hidden_pre = low_back(precise('sd,df->sf', shifted_two, up_weight) + up_bias)
    hidden = low(gelu_tanh(hidden_pre))
    feed_out = low_back(precise('sf,fd->sd', hidden, down_weight) + down_bias)
    return after_attn + modulation[5] * feed_out

def forward(latents_in, conditioning, ada_weight, ada_bias, qkv_weight, qv_bias, out_weight, out_bias, up_weight, up_bias, down_weight, down_bias):
    lifted = low(jax.nn.silu(conditioning))
    modulation = low_back(precise('bd,dje->bje', lifted, ada_weight) + ada_bias)
    weights = (qkv_weight, qv_bias, out_weight, out_bias, up_weight, up_bias, down_weight, down_bias)

    def latent_step(pair_item):
        return one_latent(pair_item[0], pair_item[1], weights)
    return lax.map(jax.checkpoint(latent_step), (latents_in, modulation))

def reference(latents_in, conditioning, ada_weight, ada_bias, qkv_weight, qv_bias, out_weight, out_bias, up_weight, up_bias, down_weight, down_bias, cotangent):
    floats = [operand.astype(jnp.float32) for operand in (latents_in, conditioning, ada_weight, ada_bias, qkv_weight, qv_bias, out_weight, out_bias, up_weight, up_bias, down_weight, down_bias)]
    output, pullback = jax.vjp(forward, *floats)
    gradients = pullback(cotangent.astype(jnp.float32))
    return (output.astype(jnp.bfloat16), gradients[0], gradients[1], gradients[2], gradients[3], gradients[4], gradients[5], gradients[6], gradients[7], gradients[8], gradients[9], gradients[10], gradients[11])
```

```python
import functools
import math

import jax
import jax.numpy as jnp
from jax import lax
from jax.experimental import pallas as pl
from jax.experimental.pallas import tpu as pltpu
from jax.sharding import PartitionSpec as P

HEAD_DIM = 64


EPSILON = 1e-06
GELU_SCALE = 0.7978845608028654
GELU_CUBIC = 0.044715

PLANE = ("fsdp", "ctx")
EVERY = ("fsdp", "ctx", "tensor")


def layer_norm(values):
    center = values - jnp.mean(values, axis=-1, keepdims=True)
    spread = jnp.mean(center * center, axis=-1, keepdims=True)
    return center * lax.rsqrt(spread + EPSILON)


def gelu_tanh(pre_act):
    return (
        0.5
        * pre_act
        * (1.0 + jnp.tanh(GELU_SCALE * (pre_act + GELU_CUBIC * pre_act * pre_act * pre_act)))
    )


def silu_slope(values):
    sigmoid_val = jax.nn.sigmoid(values)
    return sigmoid_val * (1.0 + values * (1.0 - sigmoid_val))


def total_of(sizes, axes):
    return math.prod(sizes[a] for a in axes)


def index_of(sizes, axes):
    me = 0
    for a in axes:
        me = me * sizes[a] + lax.axis_index(a)
    return me


def coords_of(sizes, axes, index):
    found = {}
    for a in reversed(axes):
        found[a] = lax.rem(index, sizes[a])
        index = lax.div(index, sizes[a])
    return {a: found[a] for a in axes}


def exchange_kernel(sizes, axes, cuts, *refs):
    count = len(cuts)
    ins, outs = refs[:count], refs[count : 2 * count]
    send_sem, recv_sem, own_sem = refs[2 * count :]
    n = total_of(sizes, axes)
    me = index_of(sizes, axes)

    barrier = pltpu.get_barrier_semaphore()

    def greet(step, carry):
        peer = lax.rem(me + step, n)
        pl.semaphore_signal(
            barrier,
            inc=1,
            device_id=coords_of(sizes, axes, peer),
            device_id_type=pl.DeviceIdType.MESH,
        )
        return carry

    lax.fori_loop(1, n, greet, 0)
    pl.semaphore_wait(barrier, n - 1)

    def copies(step):
        peer = lax.rem(me + step, n)
        return [
            pltpu.make_async_remote_copy(
                src_ref=cut_in(ins[i], peer),
                dst_ref=cut_out(outs[i], me),
                send_sem=send_sem.at[i, step - 1],
                recv_sem=recv_sem.at[i, step - 1],
                device_id=coords_of(sizes, axes, peer),
                device_id_type=pl.DeviceIdType.MESH,
            )
            for i, (cut_in, cut_out) in enumerate(cuts)
        ]

    def begin(step, carry):
        for copy in copies(step):
            copy.start()
        return carry

    def finish(step, carry):
        for copy in copies(step):
            copy.wait()
        return carry

    lax.fori_loop(1, n, begin, 0)
    own = [
        pltpu.make_async_copy(cut_in(ins[i], me), cut_out(outs[i], me), own_sem.at[i])
        for i, (cut_in, cut_out) in enumerate(cuts)
    ]
    for copy in own:
        copy.start()
    for copy in own:
        copy.wait()
    lax.fori_loop(1, n, finish, 0)


def whole_ref(ref, index):
    return ref


def lead(ref, index):
    return ref.at[index]


def rows(width):
    def cut(ref, index):
        return ref.at[:, pl.ds(pl.multiple_of(index * width, width), width), :]

    return cut


def exchange(sizes, axes, collective_id, items):
    n = total_of(sizes, axes)
    count = len(items)
    return pl.pallas_call(
        functools.partial(
            exchange_kernel, sizes, axes, [(item[1], item[2]) for item in items]
        ),
        out_shape=[jax.ShapeDtypeStruct(item[3], item[0].dtype) for item in items],
        in_specs=[pl.BlockSpec(memory_space=pl.ANY)] * count,
        out_specs=[pl.BlockSpec(memory_space=pl.ANY)] * count,
        scratch_shapes=[
            pltpu.SemaphoreType.DMA((count, n - 1)),
            pltpu.SemaphoreType.DMA((count, n - 1)),
            pltpu.SemaphoreType.DMA((count,)),
        ],
        compiler_params=pltpu.CompilerParams(
            collective_id=collective_id, has_side_effects=True
        ),
    )(*[item[0] for item in items])


def gather_item(x, n):
    return (x, whole_ref, lead, (n,) + x.shape)


def scatter_item(x):
    return (x, lead, lead, x.shape)


def gather_rows_item(x, n):
    return (x, whole_ref, rows(x.shape[1]), (x.shape[0], n * x.shape[1], x.shape[2]))


def scatter_rows_item(x, n):
    width = x.shape[1] // n
    return (x, rows(width), lead, (n, x.shape[0], width, x.shape[2]))


def body(
    sizes,
    latents_in,
    conditioning,
    ada_weight,
    ada_bias,
    qkv_weight,
    qv_bias,
    out_weight,
    out_bias,
    up_weight,
    up_bias,
    down_weight,
    down_bias,
    cotangent,
):
    f32, bf16 = jnp.float32, jnp.bfloat16
    n_fsdp, n_ctx, n_tensor = sizes["fsdp"], sizes["ctx"], sizes["tensor"]
    n_plane = n_fsdp * n_ctx
    plane_me = index_of(sizes, PLANE)
    fsdp_me = lax.axis_index("fsdp")
    tensor_me = lax.axis_index("tensor")
    latent_count, tok_rows, width = latents_in.shape
    own_rows = tok_rows // n_tensor
    depth = qkv_weight.shape[0]
    part = qkv_weight.shape[2]
    hid = up_weight.shape[1]
    local_heads = part // HEAD_DIM
    score_scale = 1.0 / math.sqrt(HEAD_DIM)

    def own(x):
        return lax.dynamic_slice_in_dim(x, tensor_me * own_rows, own_rows, 1)

    late_weights = jnp.concatenate([up_weight, down_weight.T, out_weight.T], axis=1)
    late_full = lax.all_gather(late_weights, PLANE, axis=0, tiled=True)

    cond = conditioning.astype(f32)
    biases = jnp.concatenate(
        [ada_bias.reshape(-1), qv_bias.reshape(-1), out_bias, up_bias, down_bias]
    )
    bias_len = biases.shape[0]
    bias_pad = -bias_len % 128
    biases = jnp.pad(biases.astype(f32), (0, bias_pad)).reshape(-1, 128)
    qkv_all, cond_all, bias_all = exchange(
        sizes,
        PLANE,
        1,
        [
            gather_item(qkv_weight.reshape(depth, 3 * part), n_plane),
            gather_item(cond, n_plane),
            gather_item(biases, n_plane),
        ],
    )
    qkv_full = qkv_all.reshape(width, 3 * part)
    bias_all = bias_all.reshape(n_plane, -1)
    piece = part // n_plane
    six = ada_bias.shape[0]
    at = 0
    ada_shift = bias_all[:, at : at + six * piece].reshape(n_plane, six, piece)
    ada_shift = ada_shift.transpose(1, 0, 2).reshape(six, part)
    at += six * piece
    qv_shift = bias_all[:, at : at + 2 * piece].reshape(n_plane, 2, piece)
    qv_shift = qv_shift.transpose(1, 0, 2).reshape(2, part)
    at += 2 * piece
    out_shift = bias_all[:, at : at + depth].reshape(width)
    at += depth
    up_piece = up_bias.shape[0]
    up_shift = bias_all[:, at : at + up_piece].reshape(hid)
    at += up_piece
    down_shift = bias_all[:, at : at + depth].reshape(width)

    cond_every = cond_all.reshape(n_fsdp, n_ctx, latent_count, width)[:, 0]
    cond_every = cond_every.reshape(n_fsdp * latent_count, width)
    cond_mine = lax.dynamic_slice_in_dim(cond_every, plane_me * depth, depth, 1)
    lifted_mine = jax.nn.silu(cond_mine).astype(bf16)
    ada_flat = ada_weight.reshape(depth, six * part)
    mod_terms = jnp.dot(lifted_mine, ada_flat, preferred_element_type=f32)
    mod_terms = mod_terms.reshape(n_fsdp, latent_count, six * part)

    def by_fsdp(ref, index):
        return ref.at[lax.div(index, n_ctx)]

    (mod_pieces,) = exchange(
        sizes,
        PLANE,
        2,
        [(mod_terms, by_fsdp, lead, (n_plane, latent_count, six * part))],
    )
    mod_part = jnp.sum(mod_pieces, axis=0) + ada_shift.reshape(1, six * part)
    (mod_all,) = exchange(sizes, ("tensor",), 3, [gather_item(mod_part, n_tensor)])
    modulation = (
        mod_all.reshape(n_tensor, latent_count, six, part)
        .transpose(1, 2, 0, 3)
        .reshape(latent_count, six, width)
    )
    shift_one, scale_one, gate_one, shift_two, scale_two, gate_two = [
        modulation[:, offset][:, None, :] for offset in range(6)
    ]

    inputs = latents_in.astype(f32)
    shifted = (layer_norm(inputs) * (1.0 + scale_one) + shift_one).astype(bf16)
    inputs_own = own(latents_in).astype(f32)
    normed_own, norm_back = jax.vjp(layer_norm, inputs_own)

    project = jnp.einsum("bld,de->ble", shifted, qkv_full, preferred_element_type=f32)
    queries = (project[:, :, :part] + qv_shift[0]).astype(bf16)
    keys_values = jnp.concatenate(
        [project[:, :, part : 2 * part], project[:, :, 2 * part :] + qv_shift[1]], axis=2
    ).astype(bf16)
    (kv_all,) = exchange(sizes, ("ctx",), 4, [gather_rows_item(keys_values, n_ctx)])
    seq_len = kv_all.shape[1]
    query_heads = queries.reshape(latent_count, tok_rows, local_heads, HEAD_DIM)
    key_heads = kv_all[:, :, :part].reshape(latent_count, seq_len, local_heads, HEAD_DIM)
    value_heads = kv_all[:, :, part:].reshape(latent_count, seq_len, local_heads, HEAD_DIM)
    scores = (
        jnp.einsum("bqhe,bkhe->bhqk", query_heads, key_heads, preferred_element_type=f32)
        * score_scale
    )
    log_total = jax.nn.logsumexp(scores, axis=-1, keepdims=True)
    prob_low = jnp.exp(scores - log_total).astype(bf16)
    mixed_heads = (
        jnp.einsum("bhqk,bkhe->bqhe", prob_low, value_heads, preferred_element_type=f32)
        .astype(bf16)
        .reshape(latent_count, tok_rows, part)
    )
    up_full = late_full[:, :hid]
    down_back = late_full[:, hid : 2 * hid]
    out_back = late_full[:, 2 * hid :]
    attn_part = jnp.einsum("bld,ed->ble", mixed_heads, out_back, preferred_element_type=f32)
    (attn_pieces,) = exchange(
        sizes, ("tensor",), 5, [scatter_rows_item(attn_part.astype(bf16), n_tensor)]
    )
    attended = jnp.sum(attn_pieces.astype(f32), axis=0) + out_shift
    after_attn = inputs_own + gate_one * attended
    normed_two, norm_back_two = jax.vjp(layer_norm, after_attn)
    shifted_two_own = (normed_two * (1.0 + scale_two) + shift_two).astype(bf16)
    (shifted_two,) = exchange(
        sizes, ("tensor",), 6, [gather_rows_item(shifted_two_own, n_tensor)]
    )
    hidden_pre = (
        jnp.einsum("bld,df->blf", shifted_two, up_full, preferred_element_type=f32) + up_shift
    )
    hidden_val, gelu_back = jax.vjp(gelu_tanh, hidden_pre)
    hidden = hidden_val.astype(bf16)
    feed_part = jnp.einsum("blf,df->bld", hidden, down_back, preferred_element_type=f32)
    feed_sum = lax.psum_scatter(
        feed_part.astype(bf16), "tensor", scatter_dimension=1, tiled=True
    )
    feed_out = feed_sum.astype(f32) + down_shift
    block_own = (after_attn + gate_two * feed_out).astype(bf16)
    block_out = lax.all_gather(block_own, "tensor", axis=1, tiled=True)

    upstream_own = own(cotangent).astype(f32)
    feed_grad = (gate_two * cotangent.astype(f32)).astype(bf16)
    gate_two_grad = jnp.sum(upstream_own * feed_out, axis=1)
    down_bias_grad = jnp.sum(feed_grad.astype(f32), axis=(0, 1))
    hidden_grad = jnp.einsum("bld,df->blf", feed_grad, down_back, preferred_element_type=f32)
    pre_grad = gelu_back(hidden_grad)[0].astype(bf16)
    two_part = jnp.einsum("blf,df->bld", pre_grad, up_full, preferred_element_type=f32)
    (two_pieces,) = exchange(
        sizes, ("tensor",), 7, [scatter_rows_item(two_part.astype(bf16), n_tensor)]
    )
    up_bias_grad = jnp.sum(pre_grad.astype(f32), axis=(0, 1))
    up_weight_grad = jnp.einsum(
        "bld,blf->df", shifted_two, pre_grad, preferred_element_type=f32
    )
    down_weight_grad = jnp.einsum("bld,blf->df", feed_grad, hidden, preferred_element_type=f32)
    feed_weights = jnp.concatenate(
        [up_weight_grad.astype(bf16), down_weight_grad.astype(bf16)], axis=1
    )
    feed_shard = lax.psum_scatter(feed_weights, PLANE, scatter_dimension=0, tiled=True)
    feed_shard = feed_shard.astype(f32)

    shifted_two_grad = jnp.sum(two_pieces.astype(f32), axis=0)
    scale_two_grad = jnp.sum(shifted_two_grad * normed_two, axis=1)
    shift_two_grad = jnp.sum(shifted_two_grad, axis=1)
    after_grad = upstream_own + norm_back_two(shifted_two_grad * (1.0 + scale_two))[0]
    attn_grad_own = (gate_one * after_grad).astype(bf16)
    gate_one_grad = jnp.sum(after_grad * attended, axis=1)
    (attn_grad,) = exchange(
        sizes, ("tensor",), 8, [gather_rows_item(attn_grad_own, n_tensor)]
    )
    out_bias_grad = jnp.sum(attn_grad.astype(f32), axis=(0, 1))
    out_weight_grad = jnp.einsum(
        "ble,bld->ed", attn_grad, mixed_heads, preferred_element_type=f32
    )
    mixed_grad = jnp.einsum(
        "ble,ed->bld", attn_grad, out_back, preferred_element_type=f32
    ).astype(bf16)
    mixed_grad = mixed_grad.reshape(latent_count, tok_rows, local_heads, HEAD_DIM)
    scores_again = (
        jnp.einsum("bqhe,bkhe->bhqk", query_heads, key_heads, preferred_element_type=f32)
        * score_scale
    )
    probs = jnp.exp(scores_again - log_total)
    prob_grad = jnp.einsum("bqhe,bkhe->bhqk", mixed_grad, value_heads, preferred_element_type=f32)
    row_term = jnp.sum(probs * prob_grad, axis=-1, keepdims=True)
    score_grad = (probs * (prob_grad - row_term)).astype(bf16)
    query_grad = (
        jnp.einsum("bhqk,bkhe->bqhe", score_grad, key_heads, preferred_element_type=f32)
        * score_scale
    ).astype(bf16)
    query_grad = query_grad.reshape(latent_count, tok_rows, part)
    probs_again = probs.astype(bf16)
    key_term = (
        jnp.einsum("bhqk,bqhe->bkhe", score_grad, query_heads, preferred_element_type=f32)
        * score_scale
    ).reshape(latent_count, seq_len, part)
    value_term = jnp.einsum(
        "bhqk,bqhe->bkhe", probs_again, mixed_grad, preferred_element_type=f32
    ).reshape(latent_count, seq_len, part)
    kv_term = jnp.concatenate([key_term.astype(bf16), value_term.astype(bf16)], axis=2)
    (kv_pieces,) = exchange(sizes, ("ctx",), 9, [scatter_rows_item(kv_term, n_ctx)])
    kv_grad = jnp.sum(kv_pieces.astype(f32), axis=0).astype(bf16)
    proj_grad = jnp.concatenate([query_grad, kv_grad], axis=2)
    proj_bias_grad = jnp.sum(proj_grad.astype(f32), axis=(0, 1)).reshape(3, part)
    one_part = jnp.einsum("ble,de->bld", proj_grad, qkv_full, preferred_element_type=f32)
    (one_pieces,) = exchange(
        sizes, ("tensor",), 10, [scatter_rows_item(one_part.astype(bf16), n_tensor)]
    )
    qkv_weight_grad = jnp.einsum("bld,ble->de", shifted, proj_grad, preferred_element_type=f32)

    shifted_grad = jnp.sum(one_pieces.astype(f32), axis=0)
    scale_one_grad = jnp.sum(shifted_grad * normed_own, axis=1)
    shift_one_grad = jnp.sum(shifted_grad, axis=1)
    grad_in_own = after_grad + norm_back(shifted_grad * (1.0 + scale_one))[0]
    mod_grad_own = jnp.stack(
        [
            shift_one_grad,
            scale_one_grad,
            gate_one_grad,
            shift_two_grad,
            scale_two_grad,
            gate_two_grad,
        ],
        axis=1,
    )
    mod_grad_own = (
        mod_grad_own.reshape(latent_count, six, n_tensor, part)
        .transpose(2, 0, 1, 3)
        .reshape(n_tensor, latent_count, six * part)
    )
    grad_in_all, mod_pieces_back = exchange(
        sizes,
        ("tensor",),
        11,
        [gather_rows_item(grad_in_own.astype(bf16), n_tensor), scatter_item(mod_grad_own)],
    )
    grad_in = grad_in_all.astype(f32)
    mod_grad_part = jnp.sum(mod_pieces_back, axis=0)

    bias_grads = jnp.concatenate(
        [
            proj_bias_grad[0].reshape(n_plane, piece),
            proj_bias_grad[2].reshape(n_plane, piece),
            out_bias_grad.reshape(n_plane, depth),
            up_bias_grad.reshape(n_plane, up_piece),
            down_bias_grad.reshape(n_plane, depth),
        ],
        axis=1,
    )
    bias_grads = jnp.pad(bias_grads, ((0, 0), (0, -bias_grads.shape[1] % 128)))
    bias_grads = bias_grads.reshape(n_plane, -1, 128)
    attn_weights = jnp.concatenate(
        [qkv_weight_grad.astype(bf16), out_weight_grad.astype(bf16)], axis=1
    ).reshape(n_plane, depth, 4 * part)
    weight_pieces, bias_pieces, mod_every = exchange(
        sizes,
        PLANE,
        12,
        [
            scatter_item(attn_weights),
            scatter_item(bias_grads),
            gather_item(mod_grad_part, n_plane),
        ],
    )
    attn_shard = jnp.sum(weight_pieces.astype(f32), axis=0)
    bias_shard = jnp.sum(bias_pieces, axis=0).reshape(-1)
    mod_grad = jnp.sum(
        mod_every.reshape(n_fsdp, n_ctx, latent_count, six * part), axis=1
    ).astype(bf16)
    mod_grad = mod_grad.reshape(n_fsdp * latent_count, six * part)
    ada_weight_grad = jnp.einsum(
        "bd,be->de", lifted_mine, mod_grad, preferred_element_type=f32
    ).reshape(depth, six, part)
    ada_bias_sum = jnp.sum(mod_grad.astype(f32), axis=0).reshape(six, part)
    ada_bias_grad = lax.dynamic_slice_in_dim(ada_bias_sum, plane_me * piece, piece, 1)
    lifted_part = jnp.einsum("be,de->bd", mod_grad, ada_flat, preferred_element_type=f32)
    (lifted_all,) = exchange(
        sizes, EVERY, 13, [gather_item(lifted_part, n_plane * n_tensor)]
    )
    lifted_grad = jnp.sum(
        lifted_all.reshape(n_plane, n_tensor, n_fsdp, latent_count, depth), axis=1
    )
    lifted_grad = lax.dynamic_index_in_dim(lifted_grad, fsdp_me, 1, keepdims=False)
    lifted_grad = lifted_grad.transpose(1, 0, 2).reshape(latent_count, width)
    grad_cond = lifted_grad * silu_slope(cond)

    at = 2 * piece
    out_bias_shard = bias_shard[at : at + depth]
    at += depth
    up_bias_shard = bias_shard[at : at + up_piece]
    at += up_piece
    down_bias_shard = bias_shard[at : at + depth]
    return (
        block_out,
        grad_in,
        grad_cond,
        ada_weight_grad,
        ada_bias_grad,
        attn_shard[:, : 3 * part].reshape(depth, 3, part),
        bias_shard[: 2 * piece].reshape(2, piece),
        attn_shard[:, 3 * part :].T,
        out_bias_shard,
        feed_shard[:, :hid],
        up_bias_shard,
        feed_shard[:, hid:].T,
        down_bias_shard,
    )


def solution(mesh):
    in_specs = (
        P("fsdp", "ctx", None),
        P("fsdp", None),
        P(("fsdp", "ctx"), None, "tensor"),
        P(None, ("tensor", "fsdp", "ctx")),
        P(("fsdp", "ctx"), None, "tensor"),
        P(None, ("tensor", "fsdp", "ctx")),
        P("tensor", ("fsdp", "ctx")),
        P(("fsdp", "ctx")),
        P(("fsdp", "ctx"), "tensor"),
        P(("tensor", "fsdp", "ctx")),
        P("tensor", ("fsdp", "ctx")),
        P(("fsdp", "ctx")),
        P("fsdp", "ctx", None),
    )
    out_specs = (
        P("fsdp", "ctx", None),
        P("fsdp", "ctx", None),
        P("fsdp", None),
        P(("fsdp", "ctx"), None, "tensor"),
        P(None, ("tensor", "fsdp", "ctx")),
        P(("fsdp", "ctx"), None, "tensor"),
        P(None, ("tensor", "fsdp", "ctx")),
        P("tensor", ("fsdp", "ctx")),
        P(("fsdp", "ctx")),
        P(("fsdp", "ctx"), "tensor"),
        P(("tensor", "fsdp", "ctx")),
        P("tensor", ("fsdp", "ctx")),
        P(("fsdp", "ctx")),
    )
    return jax.shard_map(functools.partial(body, dict(mesh.shape)), mesh=mesh, in_specs=in_specs, out_specs=out_specs, check_vma=False)
```

```python
import functools
import math

import jax
import jax.numpy as jnp
from jax import lax
from jax.experimental import pallas as pl
from jax.experimental.pallas import tpu as pltpu
from jax.sharding import PartitionSpec as P

HEAD_DIM = 64


EPSILON = 1e-06
GELU_SCALE = 0.7978845608028654
GELU_CUBIC = 0.044715

PLANE = ("fsdp", "ctx")
EVERY = ("fsdp", "ctx", "tensor")


def layer_norm(values):
    center = values - jnp.mean(values, axis=-1, keepdims=True)
    spread = jnp.mean(center * center, axis=-1, keepdims=True)
    return center * lax.rsqrt(spread + EPSILON)


def gelu_tanh(pre_act):
    return (
        0.5
        * pre_act
        * (1.0 + jnp.tanh(GELU_SCALE * (pre_act + GELU_CUBIC * pre_act * pre_act * pre_act)))
    )


def silu_slope(values):
    sigmoid_val = jax.nn.sigmoid(values)
    return sigmoid_val * (1.0 + values * (1.0 - sigmoid_val))


def total_of(sizes, axes):
    return math.prod(sizes[a] for a in axes)


def index_of(sizes, axes):
    me = 0
    for a in axes:
        me = me * sizes[a] + lax.axis_index(a)
    return me


def coords_of(sizes, axes, index):
    found = {}
    for a in reversed(axes):
        found[a] = lax.rem(index, sizes[a])
        index = lax.div(index, sizes[a])
    return {a: found[a] for a in axes}


def exchange_kernel(sizes, axes, cuts, *refs):
    count = len(cuts)
    ins, outs = refs[:count], refs[count : 2 * count]
    send_sem, recv_sem, own_sem = refs[2 * count :]
    n = total_of(sizes, axes)
    me = index_of(sizes, axes)

    barrier = pltpu.get_barrier_semaphore()

    def greet(step, carry):
        peer = lax.rem(me + step, n)
        pl.semaphore_signal(
            barrier,
            inc=1,
            device_id=coords_of(sizes, axes, peer),
            device_id_type=pl.DeviceIdType.MESH,
        )
        return carry

    lax.fori_loop(1, n, greet, 0)
    pl.semaphore_wait(barrier, n - 1)

    def copies(step):
        peer = lax.rem(me + step, n)
        return [
            pltpu.make_async_remote_copy(
                src_ref=cut_in(ins[i], peer),
                dst_ref=cut_out(outs[i], me),
                send_sem=send_sem.at[i, step - 1],
                recv_sem=recv_sem.at[i, step - 1],
                device_id=coords_of(sizes, axes, peer),
                device_id_type=pl.DeviceIdType.MESH,
            )
            for i, (cut_in, cut_out) in enumerate(cuts)
        ]

    def begin(step, carry):
        for copy in copies(step):
            copy.start()
        return carry

    def finish(step, carry):
        for copy in copies(step):
            copy.wait()
        return carry

    lax.fori_loop(1, n, begin, 0)
    own = [
        pltpu.make_async_copy(cut_in(ins[i], me), cut_out(outs[i], me), own_sem.at[i])
        for i, (cut_in, cut_out) in enumerate(cuts)
    ]
    for copy in own:
        copy.start()
    for copy in own:
        copy.wait()
    lax.fori_loop(1, n, finish, 0)


def whole_ref(ref, index):
    return ref


def lead(ref, index):
    return ref.at[index]


def rows(width):
    def cut(ref, index):
        return ref.at[:, pl.ds(pl.multiple_of(index * width, width), width), :]

    return cut


def exchange(sizes, axes, collective_id, items):
    n = total_of(sizes, axes)
    count = len(items)
    return pl.pallas_call(
        functools.partial(
            exchange_kernel, sizes, axes, [(item[1], item[2]) for item in items]
        ),
        out_shape=[jax.ShapeDtypeStruct(item[3], item[0].dtype) for item in items],
        in_specs=[pl.BlockSpec(memory_space=pl.ANY)] * count,
        out_specs=[pl.BlockSpec(memory_space=pl.ANY)] * count,
        scratch_shapes=[
            pltpu.SemaphoreType.DMA((count, n - 1)),
            pltpu.SemaphoreType.DMA((count, n - 1)),
            pltpu.SemaphoreType.DMA((count,)),
        ],
        compiler_params=pltpu.CompilerParams(
            collective_id=collective_id, has_side_effects=True
        ),
    )(*[item[0] for item in items])


def gather_item(x, n):
    return (x, whole_ref, lead, (n,) + x.shape)


def scatter_item(x):
    return (x, lead, lead, x.shape)


def gather_rows_item(x, n):
    return (x, whole_ref, rows(x.shape[1]), (x.shape[0], n * x.shape[1], x.shape[2]))


def scatter_rows_item(x, n):
    width = x.shape[1] // n
    return (x, rows(width), lead, (n, x.shape[0], width, x.shape[2]))


def relay_kernel(sizes, x_ref, out_ref, near_send, near_recv, far_send, far_recv, pass_send, pass_recv, own_sem):
    n = sizes["ctx"]
    half = n // 2
    blocks, width = x_ref.shape[0], x_ref.shape[1]
    me = lax.axis_index("ctx")
    mate = me + 1 - 2 * lax.rem(me, 2)

    def peer(step):
        return lax.rem(me + 2 * step, n)

    def source(step):
        return lax.rem(me + n - 2 * step, n)

    def place(block, index):
        return out_ref.at[block, pl.ds(pl.multiple_of(index * width, width), width), :]

    barrier = pltpu.get_barrier_semaphore()
    for other in [mate] + [peer(step) for step in range(1, half)]:
        pl.semaphore_signal(
            barrier, inc=1, device_id={"ctx": other}, device_id_type=pl.DeviceIdType.MESH
        )
    pl.semaphore_wait(barrier, half)

    def remote(src, dst, send, recv, other):
        return pltpu.make_async_remote_copy(
            src_ref=src,
            dst_ref=dst,
            send_sem=send,
            recv_sem=recv,
            device_id={"ctx": other},
            device_id_type=pl.DeviceIdType.MESH,
        )

    far = {}
    for block in range(blocks):
        for step in range(1, half):
            far[block, step] = remote(
                x_ref.at[block],
                place(block, me),
                far_send.at[block, step - 1],
                far_recv.at[block, step - 1],
                peer(step),
            )
            far[block, step].start()
    near = []
    for block in range(blocks):
        near.append(
            remote(x_ref.at[block], place(block, me), near_send.at[block], near_recv.at[block], mate)
        )
        near[-1].start()
    own = [
        pltpu.make_async_copy(x_ref.at[block], place(block, me), own_sem.at[block])
        for block in range(blocks)
    ]
    for copy in own:
        copy.start()
    passed = []
    for block in range(blocks):
        for step in range(1, half):
            far[block, step].wait_recv()
            landed = place(block, source(step))
            passed.append(
                remote(
                    landed,
                    landed,
                    pass_send.at[block, step - 1],
                    pass_recv.at[block, step - 1],
                    mate,
                )
            )
            passed[-1].start()
    for copy in far.values():
        copy.wait_send()
    for copy in own:
        copy.wait()
    for copy in near + passed:
        copy.wait()


def relay_gather(sizes, collective_id, x):
    n = sizes["ctx"]
    blocks = x.shape[0]
    cross = pltpu.SemaphoreType.DMA((blocks, n // 2 - 1))
    near = pltpu.SemaphoreType.DMA((blocks,))
    return pl.pallas_call(
        functools.partial(relay_kernel, sizes),
        out_shape=jax.ShapeDtypeStruct((blocks, n * x.shape[1], x.shape[2]), x.dtype),
        in_specs=[pl.BlockSpec(memory_space=pl.ANY)],
        out_specs=pl.BlockSpec(memory_space=pl.ANY),
        scratch_shapes=[near, near, cross, cross, cross, cross, near],
        compiler_params=pltpu.CompilerParams(
            collective_id=collective_id, has_side_effects=True
        ),
    )(x)


def body(
    sizes,
    latents_in,
    conditioning,
    ada_weight,
    ada_bias,
    qkv_weight,
    qv_bias,
    out_weight,
    out_bias,
    up_weight,
    up_bias,
    down_weight,
    down_bias,
    cotangent,
):
    f32, bf16 = jnp.float32, jnp.bfloat16
    n_fsdp, n_ctx, n_tensor = sizes["fsdp"], sizes["ctx"], sizes["tensor"]
    n_plane = n_fsdp * n_ctx
    plane_me = index_of(sizes, PLANE)
    fsdp_me = lax.axis_index("fsdp")
    tensor_me = lax.axis_index("tensor")
    latent_count, tok_rows, width = latents_in.shape
    own_rows = tok_rows // n_tensor
    depth = qkv_weight.shape[0]
    part = qkv_weight.shape[2]
    hid = up_weight.shape[1]
    local_heads = part // HEAD_DIM
    score_scale = 1.0 / math.sqrt(HEAD_DIM)

    def own(x):
        return lax.dynamic_slice_in_dim(x, tensor_me * own_rows, own_rows, 1)

    qkv_full = lax.all_gather(qkv_weight.reshape(depth, 3 * part), PLANE, axis=0, tiled=True)
    out_all = lax.all_gather(out_weight.T, ("tensor",) + PLANE, axis=0)
    out_back = (
        out_all.reshape(n_tensor, width, part).transpose(1, 0, 2).reshape(width, width)
    )
    late_weights = jnp.concatenate([up_weight, down_weight.T], axis=1)
    late_weights, _ = lax.optimization_barrier((late_weights, qkv_full))
    late_full = lax.all_gather(late_weights, PLANE, axis=0, tiled=True)

    cond = conditioning.astype(f32)
    biases = jnp.concatenate(
        [ada_bias.reshape(-1), qv_bias.reshape(-1), out_bias, up_bias, down_bias]
    )
    bias_len = biases.shape[0]
    bias_pad = -bias_len % 128
    biases = jnp.pad(biases.astype(f32), (0, bias_pad)).reshape(-1, 128)
    cond_all, bias_all = exchange(
        sizes,
        PLANE,
        1,
        [
            gather_item(cond, n_plane),
            gather_item(biases, n_plane),
        ],
    )
    bias_all = bias_all.reshape(n_plane, -1)
    piece = part // n_plane
    six = ada_bias.shape[0]
    at = 0
    ada_shift = bias_all[:, at : at + six * piece].reshape(n_plane, six, piece)
    ada_shift = ada_shift.transpose(1, 0, 2).reshape(six, part)
    at += six * piece
    qv_shift = bias_all[:, at : at + 2 * piece].reshape(n_plane, 2, piece)
    qv_shift = qv_shift.transpose(1, 0, 2).reshape(2, part)
    at += 2 * piece
    out_shift = bias_all[:, at : at + depth].reshape(width)
    at += depth
    up_piece = up_bias.shape[0]
    up_shift = bias_all[:, at : at + up_piece].reshape(hid)
    at += up_piece
    down_shift = bias_all[:, at : at + depth].reshape(width)

    cond_every = cond_all.reshape(n_fsdp, n_ctx, latent_count, width)[:, 0]
    cond_every = cond_every.reshape(n_fsdp * latent_count, width)
    cond_mine = lax.dynamic_slice_in_dim(cond_every, plane_me * depth, depth, 1)
    lifted_mine = jax.nn.silu(cond_mine).astype(bf16)
    ada_flat = ada_weight.reshape(depth, six * part)
    mod_terms = jnp.dot(lifted_mine, ada_flat, preferred_element_type=f32)
    mod_terms = mod_terms.reshape(n_fsdp, latent_count, six * part)

    def by_fsdp(ref, index):
        return ref.at[lax.div(index, n_ctx)]

    (mod_pieces,) = exchange(
        sizes,
        PLANE,
        2,
        [(mod_terms, by_fsdp, lead, (n_plane, latent_count, six * part))],
    )
    mod_part = jnp.sum(mod_pieces, axis=0) + ada_shift.reshape(1, six * part)
    (mod_all,) = exchange(sizes, ("tensor",), 3, [gather_item(mod_part, n_tensor)])
    modulation = (
        mod_all.reshape(n_tensor, latent_count, six, part)
        .transpose(1, 2, 0, 3)
        .reshape(latent_count, six, width)
    )
    shift_one, scale_one, gate_one, shift_two, scale_two, gate_two = [
        modulation[:, offset][:, None, :] for offset in range(6)
    ]

    inputs = latents_in.astype(f32)
    shifted = (layer_norm(inputs) * (1.0 + scale_one) + shift_one).astype(bf16)
    inputs_own = own(latents_in).astype(f32)
    normed_own, norm_back = jax.vjp(layer_norm, inputs_own)

    project = jnp.einsum("bld,de->ble", shifted, qkv_full, preferred_element_type=f32)
    queries = (project[:, :, :part] + qv_shift[0]).astype(bf16)
    keys_values = jnp.concatenate(
        [project[:, :, part : 2 * part], project[:, :, 2 * part :] + qv_shift[1]], axis=2
    ).astype(bf16)
    kv_all = relay_gather(sizes, 4, keys_values)
    seq_len = kv_all.shape[1]
    query_heads = queries.reshape(latent_count, tok_rows, local_heads, HEAD_DIM)
    key_heads = kv_all[:, :, :part].reshape(latent_count, seq_len, local_heads, HEAD_DIM)
    value_heads = kv_all[:, :, part:].reshape(latent_count, seq_len, local_heads, HEAD_DIM)
    scores = (
        jnp.einsum("bqhe,bkhe->bhqk", query_heads, key_heads, preferred_element_type=f32)
        * score_scale
    )
    log_total = jax.nn.logsumexp(scores, axis=-1, keepdims=True)
    prob_low = jnp.exp(scores - log_total).astype(bf16)
    mixed_heads = (
        jnp.einsum("bhqk,bkhe->bqhe", prob_low, value_heads, preferred_element_type=f32)
        .astype(bf16)
        .reshape(latent_count, tok_rows, part)
    )
    up_full = late_full[:, :hid]
    down_back = late_full[:, hid:]
    (mixed_pieces,) = exchange(
        sizes, ("tensor",), 5, [scatter_rows_item(mixed_heads, n_tensor)]
    )
    mixed_own = jnp.concatenate([mixed_pieces[z] for z in range(n_tensor)], axis=2)
    attended = (
        jnp.einsum("bld,ed->ble", mixed_own, out_back, preferred_element_type=f32) + out_shift
    )
    after_attn = inputs_own + gate_one * attended
    normed_two, norm_back_two = jax.vjp(layer_norm, after_attn)
    shifted_two_own = (normed_two * (1.0 + scale_two) + shift_two).astype(bf16)
    (shifted_two,) = exchange(
        sizes, ("tensor",), 6, [gather_rows_item(shifted_two_own, n_tensor)]
    )
    hidden_pre = (
        jnp.einsum("bld,df->blf", shifted_two, up_full, preferred_element_type=f32) + up_shift
    )
    hidden_val, gelu_back = jax.vjp(gelu_tanh, hidden_pre)
    hidden = hidden_val.astype(bf16)
    feed_part = jnp.einsum("blf,df->bld", hidden, down_back, preferred_element_type=f32)
    feed_sum = lax.psum_scatter(
        feed_part.astype(bf16), "tensor", scatter_dimension=1, tiled=True
    )
    feed_out = feed_sum.astype(f32) + down_shift
    block_own = (after_attn + gate_two * feed_out).astype(bf16)

    upstream_own = own(cotangent).astype(f32)
    feed_grad = (gate_two * cotangent.astype(f32)).astype(bf16)
    gate_two_grad = jnp.sum(upstream_own * feed_out, axis=1)
    down_bias_grad = jnp.sum(feed_grad.astype(f32), axis=(0, 1))
    hidden_grad = jnp.einsum("bld,df->blf", feed_grad, down_back, preferred_element_type=f32)
    pre_grad = gelu_back(hidden_grad)[0].astype(bf16)
    two_part = jnp.einsum("blf,df->bld", pre_grad, up_full, preferred_element_type=f32)
    (two_pieces,) = exchange(
        sizes, ("tensor",), 7, [scatter_rows_item(two_part.astype(bf16), n_tensor)]
    )
    up_bias_grad = jnp.sum(pre_grad.astype(f32), axis=(0, 1))
    up_weight_grad = jnp.einsum(
        "bld,blf->df", shifted_two, pre_grad, preferred_element_type=f32
    )
    down_weight_grad = jnp.einsum("bld,blf->df", feed_grad, hidden, preferred_element_type=f32)
    feed_weights = jnp.concatenate(
        [up_weight_grad.astype(bf16), down_weight_grad.astype(bf16)], axis=1
    )
    feed_shard = lax.psum_scatter(feed_weights, PLANE, scatter_dimension=0, tiled=True)
    feed_shard = feed_shard.astype(f32)

    shifted_two_grad = jnp.sum(two_pieces.astype(f32), axis=0)
    scale_two_grad = jnp.sum(shifted_two_grad * normed_two, axis=1)
    shift_two_grad = jnp.sum(shifted_two_grad, axis=1)
    after_grad = upstream_own + norm_back_two(shifted_two_grad * (1.0 + scale_two))[0]
    attn_grad_own = (gate_one * after_grad).astype(bf16)
    gate_one_grad = jnp.sum(after_grad * attended, axis=1)
    mixed_grad_own = jnp.einsum(
        "ble,ed->bld", attn_grad_own, out_back, preferred_element_type=f32
    ).astype(bf16)
    mixed_grad_cut = jnp.stack(
        [mixed_grad_own[:, :, z * part : (z + 1) * part] for z in range(n_tensor)]
    )
    mixed_grad_cut, block_own = lax.optimization_barrier((mixed_grad_cut, block_own))
    (mixed_grad,) = exchange(
        sizes,
        ("tensor",),
        8,
        [(mixed_grad_cut, lead, rows(own_rows), (latent_count, tok_rows, part))],
    )
    block_out = lax.all_gather(block_own, "tensor", axis=1, tiled=True)
    out_bias_part = jnp.sum(attn_grad_own.astype(f32), axis=(0, 1))
    out_weight_part = jnp.einsum(
        "zbld,ble->zde", mixed_pieces, attn_grad_own, preferred_element_type=f32
    ).astype(bf16)
    out_weight_grad = lax.psum_scatter(
        out_weight_part.reshape(width, width), "tensor", scatter_dimension=0, tiled=True
    ).T
    mixed_grad = mixed_grad.reshape(latent_count, tok_rows, local_heads, HEAD_DIM)
    scores_again = (
        jnp.einsum("bqhe,bkhe->bhqk", query_heads, key_heads, preferred_element_type=f32)
        * score_scale
    )
    probs = jnp.exp(scores_again - log_total)
    prob_grad = jnp.einsum("bqhe,bkhe->bhqk", mixed_grad, value_heads, preferred_element_type=f32)
    row_term = jnp.sum(probs * prob_grad, axis=-1, keepdims=True)
    score_grad = (probs * (prob_grad - row_term)).astype(bf16)
    query_grad = (
        jnp.einsum("bhqk,bkhe->bqhe", score_grad, key_heads, preferred_element_type=f32)
        * score_scale
    ).astype(bf16)
    query_grad = query_grad.reshape(latent_count, tok_rows, part)
    probs_again = probs.astype(bf16)
    key_term = (
        jnp.einsum("bhqk,bqhe->bkhe", score_grad, query_heads, preferred_element_type=f32)
        * score_scale
    ).reshape(latent_count, seq_len, part)
    value_term = jnp.einsum(
        "bhqk,bqhe->bkhe", probs_again, mixed_grad, preferred_element_type=f32
    ).reshape(latent_count, seq_len, part)
    kv_term = jnp.concatenate([key_term.astype(bf16), value_term.astype(bf16)], axis=2)
    (kv_pieces,) = exchange(sizes, ("ctx",), 9, [scatter_rows_item(kv_term, n_ctx)])
    kv_grad = jnp.sum(kv_pieces.astype(f32), axis=0).astype(bf16)
    proj_grad = jnp.concatenate([query_grad, kv_grad], axis=2)
    proj_bias_grad = jnp.sum(proj_grad.astype(f32), axis=(0, 1)).reshape(3, part)
    one_part = jnp.einsum("ble,de->bld", proj_grad, qkv_full, preferred_element_type=f32)
    (one_pieces,) = exchange(
        sizes, ("tensor",), 10, [scatter_rows_item(one_part.astype(bf16), n_tensor)]
    )
    qkv_weight_grad = jnp.einsum("bld,ble->de", shifted, proj_grad, preferred_element_type=f32)

    shifted_grad = jnp.sum(one_pieces.astype(f32), axis=0)
    scale_one_grad = jnp.sum(shifted_grad * normed_own, axis=1)
    shift_one_grad = jnp.sum(shifted_grad, axis=1)
    grad_in_own = after_grad + norm_back(shifted_grad * (1.0 + scale_one))[0]
    mod_grad_own = jnp.stack(
        [
            shift_one_grad,
            scale_one_grad,
            gate_one_grad,
            shift_two_grad,
            scale_two_grad,
            gate_two_grad,
        ],
        axis=1,
    )
    mod_grad_own = (
        mod_grad_own.reshape(latent_count, six, n_tensor, part)
        .transpose(2, 0, 1, 3)
        .reshape(n_tensor, latent_count, six * part)
    )
    mod_pieces_back, out_bias_pieces = exchange(
        sizes,
        ("tensor",),
        11,
        [scatter_item(mod_grad_own), gather_item(out_bias_part.reshape(-1, 128), n_tensor)],
    )
    grad_in_low = grad_in_own.astype(bf16)
    grad_in = lax.all_gather(grad_in_low, "tensor", axis=1, tiled=True).astype(f32)
    mod_grad_part = jnp.sum(mod_pieces_back, axis=0)
    out_bias_grad = jnp.sum(out_bias_pieces, axis=0).reshape(width)

    bias_grads = jnp.concatenate(
        [
            proj_bias_grad[0].reshape(n_plane, piece),
            proj_bias_grad[2].reshape(n_plane, piece),
            out_bias_grad.reshape(n_plane, depth),
            up_bias_grad.reshape(n_plane, up_piece),
            down_bias_grad.reshape(n_plane, depth),
        ],
        axis=1,
    )
    bias_grads = jnp.pad(bias_grads, ((0, 0), (0, -bias_grads.shape[1] % 128)))
    bias_grads = bias_grads.reshape(n_plane, -1, 128)
    attn_weights = jnp.concatenate(
        [qkv_weight_grad.astype(bf16), out_weight_grad.astype(bf16)], axis=1
    ).reshape(n_plane, depth, 4 * part)
    weight_pieces, bias_pieces, mod_every = exchange(
        sizes,
        PLANE,
        12,
        [
            scatter_item(attn_weights),
            scatter_item(bias_grads),
            gather_item(mod_grad_part, n_plane),
        ],
    )
    attn_shard = jnp.sum(weight_pieces.astype(f32), axis=0)
    bias_shard = jnp.sum(bias_pieces, axis=0).reshape(-1)
    mod_grad = jnp.sum(
        mod_every.reshape(n_fsdp, n_ctx, latent_count, six * part), axis=1
    ).astype(bf16)
    mod_grad = mod_grad.reshape(n_fsdp * latent_count, six * part)
    ada_weight_grad = jnp.einsum(
        "bd,be->de", lifted_mine, mod_grad, preferred_element_type=f32
    ).reshape(depth, six, part)
    ada_bias_sum = jnp.sum(mod_grad.astype(f32), axis=0).reshape(six, part)
    ada_bias_grad = lax.dynamic_slice_in_dim(ada_bias_sum, plane_me * piece, piece, 1)
    lifted_part = jnp.einsum("be,de->bd", mod_grad, ada_flat, preferred_element_type=f32)
    (lifted_all,) = exchange(
        sizes, EVERY, 13, [gather_item(lifted_part, n_plane * n_tensor)]
    )
    lifted_grad = jnp.sum(
        lifted_all.reshape(n_plane, n_tensor, n_fsdp, latent_count, depth), axis=1
    )
    lifted_grad = lax.dynamic_index_in_dim(lifted_grad, fsdp_me, 1, keepdims=False)
    lifted_grad = lifted_grad.transpose(1, 0, 2).reshape(latent_count, width)
    grad_cond = lifted_grad * silu_slope(cond)

    at = 2 * piece
    out_bias_shard = bias_shard[at : at + depth]
    at += depth
    up_bias_shard = bias_shard[at : at + up_piece]
    at += up_piece
    down_bias_shard = bias_shard[at : at + depth]
    return (
        block_out,
        grad_in,
        grad_cond,
        ada_weight_grad,
        ada_bias_grad,
        attn_shard[:, : 3 * part].reshape(depth, 3, part),
        bias_shard[: 2 * piece].reshape(2, piece),
        attn_shard[:, 3 * part :].T,
        out_bias_shard,
        feed_shard[:, :hid],
        up_bias_shard,
        feed_shard[:, hid:].T,
        down_bias_shard,
    )


def solution(mesh):
    in_specs = (
        P("fsdp", "ctx", None),
        P("fsdp", None),
        P(("fsdp", "ctx"), None, "tensor"),
        P(None, ("tensor", "fsdp", "ctx")),
        P(("fsdp", "ctx"), None, "tensor"),
        P(None, ("tensor", "fsdp", "ctx")),
        P("tensor", ("fsdp", "ctx")),
        P(("fsdp", "ctx")),
        P(("fsdp", "ctx"), "tensor"),
        P(("tensor", "fsdp", "ctx")),
        P("tensor", ("fsdp", "ctx")),
        P(("fsdp", "ctx")),
        P("fsdp", "ctx", None),
    )
    out_specs = (
        P("fsdp", "ctx", None),
        P("fsdp", "ctx", None),
        P("fsdp", None),
        P(("fsdp", "ctx"), None, "tensor"),
        P(None, ("tensor", "fsdp", "ctx")),
        P(("fsdp", "ctx"), None, "tensor"),
        P(None, ("tensor", "fsdp", "ctx")),
        P("tensor", ("fsdp", "ctx")),
        P(("fsdp", "ctx")),
        P(("fsdp", "ctx"), "tensor"),
        P(("tensor", "fsdp", "ctx")),
        P("tensor", ("fsdp", "ctx")),
        P(("fsdp", "ctx")),
    )
    return jax.shard_map(functools.partial(body, dict(mesh.shape)), mesh=mesh, in_specs=in_specs, out_specs=out_specs, check_vma=False)
```

```python
import functools
import math

import jax
import jax.numpy as jnp
from jax import lax
from jax.experimental import pallas as pl
from jax.experimental.pallas import tpu as pltpu
from jax.sharding import PartitionSpec as P

HEAD_DIM = 64


EPSILON = 1e-06
GELU_SCALE = 0.7978845608028654
GELU_CUBIC = 0.044715

PLANE = ("fsdp", "ctx")
EVERY = ("fsdp", "ctx", "tensor")


def layer_norm(values):
    center = values - jnp.mean(values, axis=-1, keepdims=True)
    spread = jnp.mean(center * center, axis=-1, keepdims=True)
    return center * lax.rsqrt(spread + EPSILON)


def gelu_tanh(pre_act):
    return (
        0.5
        * pre_act
        * (1.0 + jnp.tanh(GELU_SCALE * (pre_act + GELU_CUBIC * pre_act * pre_act * pre_act)))
    )


def silu_slope(values):
    sigmoid_val = jax.nn.sigmoid(values)
    return sigmoid_val * (1.0 + values * (1.0 - sigmoid_val))


def total_of(sizes, axes):
    return math.prod(sizes[a] for a in axes)


def index_of(sizes, axes):
    me = 0
    for a in axes:
        me = me * sizes[a] + lax.axis_index(a)
    return me


def coords_of(sizes, axes, index):
    found = {}
    for a in reversed(axes):
        found[a] = lax.rem(index, sizes[a])
        index = lax.div(index, sizes[a])
    return {a: found[a] for a in axes}


def exchange_kernel(sizes, groups, *refs):
    count = sum(len(cuts) for _, cuts in groups)
    ins, outs = refs[:count], refs[count : 2 * count]
    sems = refs[2 * count :]
    barrier = pltpu.get_barrier_semaphore()

    def neighbours(axes):
        n = total_of(sizes, axes)
        me = index_of(sizes, axes)

        def peer_of(step):
            return lax.rem(me + step, n)

        return n, me, peer_of

    for axes, _ in groups:
        n, me, peer_of = neighbours(axes)

        def greet(step, carry, axes=axes, peer_of=peer_of):
            pl.semaphore_signal(
                barrier,
                inc=1,
                device_id=coords_of(sizes, axes, peer_of(step)),
                device_id_type=pl.DeviceIdType.MESH,
            )
            return carry

        lax.fori_loop(1, n, greet, 0)
    pl.semaphore_wait(barrier, sum(total_of(sizes, axes) - 1 for axes, _ in groups))

    pending = []
    own = []
    first = 0
    for place, (axes, cuts) in enumerate(groups):
        n, me, peer_of = neighbours(axes)
        send_sem, recv_sem, own_sem = sems[3 * place : 3 * place + 3]

        def copies(step, axes=axes, cuts=cuts, first=first, me=me, peer_of=peer_of, sends=send_sem, recvs=recv_sem):
            peer = peer_of(step)
            return [
                pltpu.make_async_remote_copy(
                    src_ref=cut_in(ins[first + i], peer),
                    dst_ref=cut_out(outs[first + i], me),
                    send_sem=sends.at[i, step - 1],
                    recv_sem=recvs.at[i, step - 1],
                    device_id=coords_of(sizes, axes, peer),
                    device_id_type=pl.DeviceIdType.MESH,
                )
                for i, (cut_in, cut_out) in enumerate(cuts)
            ]

        def begin(step, carry, copies=copies):
            for copy in copies(step):
                copy.start()
            return carry

        def finish(step, carry, copies=copies):
            for copy in copies(step):
                copy.wait()
            return carry

        lax.fori_loop(1, n, begin, 0)
        pending.append((n, finish))
        own += [
            pltpu.make_async_copy(
                cut_in(ins[first + i], me), cut_out(outs[first + i], me), own_sem.at[i]
            )
            for i, (cut_in, cut_out) in enumerate(cuts)
        ]
        first += len(cuts)
    for copy in own:
        copy.start()
    for copy in own:
        copy.wait()
    for n, finish in pending:
        lax.fori_loop(1, n, finish, 0)


def whole_ref(ref, index):
    return ref


def lead(ref, index):
    return ref.at[index]


def rows(width):
    def cut(ref, index):
        return ref.at[:, pl.ds(pl.multiple_of(index * width, width), width), :]

    return cut


def exchange(sizes, axes, collective_id, items, more=()):
    groups = [(axes, items)] + list(more)
    every = [item for _, members in groups for item in members]
    scratch = []
    for near, members in groups:
        pairs = pltpu.SemaphoreType.DMA((len(members), total_of(sizes, near) - 1))
        scratch += [pairs, pairs, pltpu.SemaphoreType.DMA((len(members),))]
    return pl.pallas_call(
        functools.partial(
            exchange_kernel,
            sizes,
            [(near, [(item[1], item[2]) for item in members]) for near, members in groups],
        ),
        out_shape=[jax.ShapeDtypeStruct(item[3], item[0].dtype) for item in every],
        in_specs=[pl.BlockSpec(memory_space=pl.ANY)] * len(every),
        out_specs=[pl.BlockSpec(memory_space=pl.ANY)] * len(every),
        scratch_shapes=scratch,
        compiler_params=pltpu.CompilerParams(
            collective_id=collective_id, has_side_effects=True
        ),
    )(*[item[0] for item in every])


def gather_item(x, n):
    return (x, whole_ref, lead, (n,) + x.shape)


def scatter_item(x):
    return (x, lead, lead, x.shape)


def gather_rows_item(x, n):
    return (x, whole_ref, rows(x.shape[1]), (x.shape[0], n * x.shape[1], x.shape[2]))


def scatter_rows_item(x, n):
    width = x.shape[1] // n
    return (x, rows(width), lead, (n, x.shape[0], width, x.shape[2]))


def relay_kernel(sizes, x_ref, out_ref, near_send, near_recv, far_send, far_recv, pass_send, pass_recv, own_sem):
    n = sizes["ctx"]
    half = n // 2
    blocks, width = x_ref.shape[0], x_ref.shape[1]
    me = lax.axis_index("ctx")
    mate = me + 1 - 2 * lax.rem(me, 2)

    def peer(step):
        return lax.rem(me + 2 * step, n)

    def source(step):
        return lax.rem(me + n - 2 * step, n)

    def place(block, index):
        return out_ref.at[block, pl.ds(pl.multiple_of(index * width, width), width), :]

    barrier = pltpu.get_barrier_semaphore()
    for other in [mate] + [peer(step) for step in range(1, half)]:
        pl.semaphore_signal(
            barrier, inc=1, device_id={"ctx": other}, device_id_type=pl.DeviceIdType.MESH
        )
    pl.semaphore_wait(barrier, half)

    def remote(src, dst, send, recv, other):
        return pltpu.make_async_remote_copy(
            src_ref=src,
            dst_ref=dst,
            send_sem=send,
            recv_sem=recv,
            device_id={"ctx": other},
            device_id_type=pl.DeviceIdType.MESH,
        )

    far = {}
    for block in range(blocks):
        for step in range(1, half):
            far[block, step] = remote(
                x_ref.at[block],
                place(block, me),
                far_send.at[block, step - 1],
                far_recv.at[block, step - 1],
                peer(step),
            )
            far[block, step].start()
    near = []
    for block in range(blocks):
        near.append(
            remote(x_ref.at[block], place(block, me), near_send.at[block], near_recv.at[block], mate)
        )
        near[-1].start()
    own = [
        pltpu.make_async_copy(x_ref.at[block], place(block, me), own_sem.at[block])
        for block in range(blocks)
    ]
    for copy in own:
        copy.start()
    passed = []
    for block in range(blocks):
        for step in range(1, half):
            far[block, step].wait_recv()
            landed = place(block, source(step))
            passed.append(
                remote(
                    landed,
                    landed,
                    pass_send.at[block, step - 1],
                    pass_recv.at[block, step - 1],
                    mate,
                )
            )
            passed[-1].start()
    for copy in far.values():
        copy.wait_send()
    for copy in own:
        copy.wait()
    for copy in near + passed:
        copy.wait()


def relay_gather(sizes, collective_id, x):
    n = sizes["ctx"]
    blocks = x.shape[0]
    cross = pltpu.SemaphoreType.DMA((blocks, n // 2 - 1))
    near = pltpu.SemaphoreType.DMA((blocks,))
    return pl.pallas_call(
        functools.partial(relay_kernel, sizes),
        out_shape=jax.ShapeDtypeStruct((blocks, n * x.shape[1], x.shape[2]), x.dtype),
        in_specs=[pl.BlockSpec(memory_space=pl.ANY)],
        out_specs=pl.BlockSpec(memory_space=pl.ANY),
        scratch_shapes=[near, near, cross, cross, cross, cross, near],
        compiler_params=pltpu.CompilerParams(
            collective_id=collective_id, has_side_effects=True
        ),
    )(x)


def body(
    sizes,
    latents_in,
    conditioning,
    ada_weight,
    ada_bias,
    qkv_weight,
    qv_bias,
    out_weight,
    out_bias,
    up_weight,
    up_bias,
    down_weight,
    down_bias,
    cotangent,
):
    f32, bf16 = jnp.float32, jnp.bfloat16
    n_fsdp, n_ctx, n_tensor = sizes["fsdp"], sizes["ctx"], sizes["tensor"]
    n_plane = n_fsdp * n_ctx
    plane_me = index_of(sizes, PLANE)
    fsdp_me = lax.axis_index("fsdp")
    tensor_me = lax.axis_index("tensor")
    latent_count, tok_rows, width = latents_in.shape
    own_rows = tok_rows // n_tensor
    depth = qkv_weight.shape[0]
    part = qkv_weight.shape[2]
    hid = up_weight.shape[1]
    local_heads = part // HEAD_DIM
    score_scale = 1.0 / math.sqrt(HEAD_DIM)

    def own(x):
        return lax.dynamic_slice_in_dim(x, tensor_me * own_rows, own_rows, 1)

    out_all = lax.all_gather(out_weight.T, ("tensor",) + PLANE, axis=0)
    out_back = (
        out_all.reshape(n_tensor, width, part).transpose(1, 0, 2).reshape(width, width)
    )

    cond = conditioning.astype(f32)
    biases = jnp.concatenate(
        [ada_bias.reshape(-1), qv_bias.reshape(-1), out_bias, up_bias, down_bias]
    )
    bias_len = biases.shape[0]
    bias_pad = -bias_len % 128
    biases = jnp.pad(biases.astype(f32), (0, bias_pad)).reshape(-1, 128)
    cond_all, bias_all = exchange(
        sizes,
        PLANE,
        1,
        [
            gather_item(cond, n_plane),
            gather_item(biases, n_plane),
        ],
    )
    bias_all = bias_all.reshape(n_plane, -1)
    piece = part // n_plane
    six = ada_bias.shape[0]
    at = 0
    ada_shift = bias_all[:, at : at + six * piece].reshape(n_plane, six, piece)
    ada_shift = ada_shift.transpose(1, 0, 2).reshape(six, part)
    at += six * piece
    qv_shift = bias_all[:, at : at + 2 * piece].reshape(n_plane, 2, piece)
    qv_shift = qv_shift.transpose(1, 0, 2).reshape(2, part)
    at += 2 * piece
    out_shift = bias_all[:, at : at + depth].reshape(width)
    at += depth
    up_piece = up_bias.shape[0]
    up_shift = bias_all[:, at : at + up_piece].reshape(hid)
    at += up_piece
    down_shift = bias_all[:, at : at + depth].reshape(width)

    cond_every = cond_all.reshape(n_fsdp, n_ctx, latent_count, width)[:, 0]
    cond_every = cond_every.reshape(n_fsdp * latent_count, width)
    cond_mine = lax.dynamic_slice_in_dim(cond_every, plane_me * depth, depth, 1)
    lifted_mine = jax.nn.silu(cond_mine).astype(bf16)
    ada_flat = ada_weight.reshape(depth, six * part)
    mod_terms = jnp.dot(lifted_mine, ada_flat, preferred_element_type=f32)
    mod_terms = mod_terms.reshape(n_fsdp, latent_count, six * part)

    def by_fsdp(ref, index):
        return ref.at[lax.div(index, n_ctx)]

    (mod_pieces,) = exchange(
        sizes,
        PLANE,
        2,
        [(mod_terms, by_fsdp, lead, (n_plane, latent_count, six * part))],
    )
    mod_part = jnp.sum(mod_pieces, axis=0) + ada_shift.reshape(1, six * part)
    mod_all, qkv_all = exchange(
        sizes,
        ("tensor",),
        3,
        [gather_item(mod_part, n_tensor)],
        [(PLANE, [gather_item(qkv_weight.reshape(depth, 3 * part), n_plane)])],
    )
    qkv_full = qkv_all.reshape(width, 3 * part)
    late_weights = jnp.concatenate([up_weight, down_weight.T], axis=1)
    late_weights, _ = lax.optimization_barrier((late_weights, qkv_all))
    late_full = lax.all_gather(late_weights, PLANE, axis=0, tiled=True)
    modulation = (
        mod_all.reshape(n_tensor, latent_count, six, part)
        .transpose(1, 2, 0, 3)
        .reshape(latent_count, six, width)
    )
    shift_one, scale_one, gate_one, shift_two, scale_two, gate_two = [
        modulation[:, offset][:, None, :] for offset in range(6)
    ]

    inputs = latents_in.astype(f32)
    shifted = (layer_norm(inputs) * (1.0 + scale_one) + shift_one).astype(bf16)
    inputs_own = own(latents_in).astype(f32)
    normed_own, norm_back = jax.vjp(layer_norm, inputs_own)

    project = jnp.einsum("bld,de->ble", shifted, qkv_full, preferred_element_type=f32)
    queries = (project[:, :, :part] + qv_shift[0]).astype(bf16)
    keys_values = jnp.concatenate(
        [project[:, :, part : 2 * part], project[:, :, 2 * part :] + qv_shift[1]], axis=2
    ).astype(bf16)
    kv_all = relay_gather(sizes, 4, keys_values)
    seq_len = kv_all.shape[1]
    query_heads = queries.reshape(latent_count, tok_rows, local_heads, HEAD_DIM)
    key_heads = kv_all[:, :, :part].reshape(latent_count, seq_len, local_heads, HEAD_DIM)
    value_heads = kv_all[:, :, part:].reshape(latent_count, seq_len, local_heads, HEAD_DIM)
    scores = (
        jnp.einsum("bqhe,bkhe->bhqk", query_heads, key_heads, preferred_element_type=f32)
        * score_scale
    )
    log_total = jax.nn.logsumexp(scores, axis=-1, keepdims=True)
    prob_low = jnp.exp(scores - log_total).astype(bf16)
    mixed_heads = (
        jnp.einsum("bhqk,bkhe->bqhe", prob_low, value_heads, preferred_element_type=f32)
        .astype(bf16)
        .reshape(latent_count, tok_rows, part)
    )
    up_full = late_full[:, :hid]
    down_back = late_full[:, hid:]
    (mixed_pieces,) = exchange(
        sizes, ("tensor",), 5, [scatter_rows_item(mixed_heads, n_tensor)]
    )
    mixed_own = jnp.concatenate([mixed_pieces[z] for z in range(n_tensor)], axis=2)
    attended = (
        jnp.einsum("bld,ed->ble", mixed_own, out_back, preferred_element_type=f32) + out_shift
    )
    after_attn = inputs_own + gate_one * attended
    normed_two, norm_back_two = jax.vjp(layer_norm, after_attn)
    shifted_two_own = (normed_two * (1.0 + scale_two) + shift_two).astype(bf16)
    (shifted_two,) = exchange(
        sizes, ("tensor",), 6, [gather_rows_item(shifted_two_own, n_tensor)]
    )
    hidden_pre = (
        jnp.einsum("bld,df->blf", shifted_two, up_full, preferred_element_type=f32) + up_shift
    )
    hidden_val, gelu_back = jax.vjp(gelu_tanh, hidden_pre)
    hidden = hidden_val.astype(bf16)
    feed_part = jnp.einsum("blf,df->bld", hidden, down_back, preferred_element_type=f32)
    feed_sum = lax.psum_scatter(
        feed_part.astype(bf16), "tensor", scatter_dimension=1, tiled=True
    )
    feed_out = feed_sum.astype(f32) + down_shift
    block_own = (after_attn + gate_two * feed_out).astype(bf16)

    upstream_own = own(cotangent).astype(f32)
    feed_grad = (gate_two * cotangent.astype(f32)).astype(bf16)
    gate_two_grad = jnp.sum(upstream_own * feed_out, axis=1)
    down_bias_grad = jnp.sum(feed_grad.astype(f32), axis=(0, 1))
    hidden_grad = jnp.einsum("bld,df->blf", feed_grad, down_back, preferred_element_type=f32)
    pre_grad = gelu_back(hidden_grad)[0].astype(bf16)
    two_part = jnp.einsum("blf,df->bld", pre_grad, up_full, preferred_element_type=f32)
    (two_pieces,) = exchange(
        sizes, ("tensor",), 7, [scatter_rows_item(two_part.astype(bf16), n_tensor)]
    )
    up_bias_grad = jnp.sum(pre_grad.astype(f32), axis=(0, 1))
    up_weight_grad = jnp.einsum(
        "bld,blf->df", shifted_two, pre_grad, preferred_element_type=f32
    )
    down_weight_grad = jnp.einsum("bld,blf->df", feed_grad, hidden, preferred_element_type=f32)
    feed_weights = jnp.concatenate(
        [up_weight_grad.astype(bf16), down_weight_grad.astype(bf16)], axis=1
    )
    feed_weights = feed_weights.reshape(n_plane, depth, 2 * hid)

    shifted_two_grad = jnp.sum(two_pieces.astype(f32), axis=0)
    scale_two_grad = jnp.sum(shifted_two_grad * normed_two, axis=1)
    shift_two_grad = jnp.sum(shifted_two_grad, axis=1)
    after_grad = upstream_own + norm_back_two(shifted_two_grad * (1.0 + scale_two))[0]
    attn_grad_own = (gate_one * after_grad).astype(bf16)
    gate_one_grad = jnp.sum(after_grad * attended, axis=1)
    mixed_grad_own = jnp.einsum(
        "ble,ed->bld", attn_grad_own, out_back, preferred_element_type=f32
    ).astype(bf16)
    mixed_grad_cut = jnp.stack(
        [mixed_grad_own[:, :, z * part : (z + 1) * part] for z in range(n_tensor)]
    )
    mixed_grad_cut, block_own = lax.optimization_barrier((mixed_grad_cut, block_own))
    (mixed_grad,) = exchange(
        sizes,
        ("tensor",),
        8,
        [(mixed_grad_cut, lead, rows(own_rows), (latent_count, tok_rows, part))],
    )
    block_out = lax.all_gather(block_own, "tensor", axis=1, tiled=True)
    out_bias_part = jnp.sum(attn_grad_own.astype(f32), axis=(0, 1))
    out_weight_part = jnp.einsum(
        "zbld,ble->zde", mixed_pieces, attn_grad_own, preferred_element_type=f32
    ).astype(bf16)
    out_weight_grad = lax.psum_scatter(
        out_weight_part.reshape(width, width), "tensor", scatter_dimension=0, tiled=True
    ).T
    mixed_grad = mixed_grad.reshape(latent_count, tok_rows, local_heads, HEAD_DIM)
    scores_again = (
        jnp.einsum("bqhe,bkhe->bhqk", query_heads, key_heads, preferred_element_type=f32)
        * score_scale
    )
    probs = jnp.exp(scores_again - log_total)
    prob_grad = jnp.einsum("bqhe,bkhe->bhqk", mixed_grad, value_heads, preferred_element_type=f32)
    row_term = jnp.sum(probs * prob_grad, axis=-1, keepdims=True)
    score_grad = (probs * (prob_grad - row_term)).astype(bf16)
    query_grad = (
        jnp.einsum("bhqk,bkhe->bqhe", score_grad, key_heads, preferred_element_type=f32)
        * score_scale
    ).astype(bf16)
    query_grad = query_grad.reshape(latent_count, tok_rows, part)
    probs_again = probs.astype(bf16)
    key_term = (
        jnp.einsum("bhqk,bqhe->bkhe", score_grad, query_heads, preferred_element_type=f32)
        * score_scale
    ).reshape(latent_count, seq_len, part)
    value_term = jnp.einsum(
        "bhqk,bqhe->bkhe", probs_again, mixed_grad, preferred_element_type=f32
    ).reshape(latent_count, seq_len, part)
    kv_term = jnp.concatenate([key_term.astype(bf16), value_term.astype(bf16)], axis=2)
    kv_term, block_out = lax.optimization_barrier((kv_term, block_out))
    (kv_pieces,) = exchange(sizes, ("ctx",), 9, [scatter_rows_item(kv_term, n_ctx)])
    kv_grad = jnp.sum(kv_pieces.astype(f32), axis=0).astype(bf16)
    proj_grad = jnp.concatenate([query_grad, kv_grad], axis=2)
    proj_bias_grad = jnp.sum(proj_grad.astype(f32), axis=(0, 1)).reshape(3, part)
    one_part = jnp.einsum("ble,de->bld", proj_grad, qkv_full, preferred_element_type=f32)
    one_low, out_weight_grad = lax.optimization_barrier(
        (one_part.astype(bf16), out_weight_grad)
    )
    one_pieces, feed_pieces = exchange(
        sizes,
        ("tensor",),
        10,
        [scatter_rows_item(one_low, n_tensor)],
        [(PLANE, [scatter_item(feed_weights)])],
    )
    feed_shard = jnp.sum(feed_pieces.astype(f32), axis=0)
    qkv_weight_grad = jnp.einsum("bld,ble->de", shifted, proj_grad, preferred_element_type=f32)

    shifted_grad = jnp.sum(one_pieces.astype(f32), axis=0)
    scale_one_grad = jnp.sum(shifted_grad * normed_own, axis=1)
    shift_one_grad = jnp.sum(shifted_grad, axis=1)
    grad_in_own = after_grad + norm_back(shifted_grad * (1.0 + scale_one))[0]
    mod_grad_own = jnp.stack(
        [
            shift_one_grad,
            scale_one_grad,
            gate_one_grad,
            shift_two_grad,
            scale_two_grad,
            gate_two_grad,
        ],
        axis=1,
    )
    mod_grad_own = (
        mod_grad_own.reshape(latent_count, six, n_tensor, part)
        .transpose(2, 0, 1, 3)
        .reshape(n_tensor, latent_count, six * part)
    )
    bias_grads = jnp.concatenate(
        [
            proj_bias_grad[0].reshape(n_plane, piece),
            proj_bias_grad[2].reshape(n_plane, piece),
            up_bias_grad.reshape(n_plane, up_piece),
            down_bias_grad.reshape(n_plane, depth),
        ],
        axis=1,
    )
    bias_grads = jnp.pad(bias_grads, ((0, 0), (0, -bias_grads.shape[1] % 128)))
    bias_grads = bias_grads.reshape(n_plane, -1, 128)
    attn_weights = jnp.concatenate(
        [qkv_weight_grad.astype(bf16), out_weight_grad.astype(bf16)], axis=1
    ).reshape(n_plane, depth, 4 * part)
    mod_pieces_back, out_bias_pieces, weight_pieces, bias_pieces = exchange(
        sizes,
        ("tensor",),
        11,
        [scatter_item(mod_grad_own), gather_item(out_bias_part.reshape(-1, 128), n_tensor)],
        [(PLANE, [scatter_item(attn_weights), scatter_item(bias_grads)])],
    )
    grad_in_low = grad_in_own.astype(bf16)
    grad_in = lax.all_gather(grad_in_low, "tensor", axis=1, tiled=True).astype(f32)
    mod_grad_part = jnp.sum(mod_pieces_back, axis=0)
    out_bias_grad = jnp.sum(out_bias_pieces, axis=0).reshape(n_plane, depth)
    mod_every, out_bias_every = exchange(
        sizes,
        PLANE,
        12,
        [
            gather_item(mod_grad_part, n_plane),
            scatter_item(out_bias_grad.reshape(n_plane, 1, depth)),
        ],
    )
    attn_shard = jnp.sum(weight_pieces.astype(f32), axis=0)
    bias_shard = jnp.sum(bias_pieces, axis=0).reshape(-1)
    mod_grad = jnp.sum(
        mod_every.reshape(n_fsdp, n_ctx, latent_count, six * part), axis=1
    ).astype(bf16)
    mod_grad = mod_grad.reshape(n_fsdp * latent_count, six * part)
    ada_weight_grad = jnp.einsum(
        "bd,be->de", lifted_mine, mod_grad, preferred_element_type=f32
    ).reshape(depth, six, part)
    ada_bias_sum = jnp.sum(mod_grad.astype(f32), axis=0).reshape(six, part)
    ada_bias_grad = lax.dynamic_slice_in_dim(ada_bias_sum, plane_me * piece, piece, 1)
    lifted_part = jnp.einsum("be,de->bd", mod_grad, ada_flat, preferred_element_type=f32)
    (lifted_all,) = exchange(
        sizes, EVERY, 13, [gather_item(lifted_part, n_plane * n_tensor)]
    )
    lifted_grad = jnp.sum(
        lifted_all.reshape(n_plane, n_tensor, n_fsdp, latent_count, depth), axis=1
    )
    lifted_grad = lax.dynamic_index_in_dim(lifted_grad, fsdp_me, 1, keepdims=False)
    lifted_grad = lifted_grad.transpose(1, 0, 2).reshape(latent_count, width)
    grad_cond = lifted_grad * silu_slope(cond)

    at = 2 * piece
    out_bias_shard = jnp.sum(out_bias_every, axis=0).reshape(depth)
    up_bias_shard = bias_shard[at : at + up_piece]
    at += up_piece
    down_bias_shard = bias_shard[at : at + depth]
    return (
        block_out,
        grad_in,
        grad_cond,
        ada_weight_grad,
        ada_bias_grad,
        attn_shard[:, : 3 * part].reshape(depth, 3, part),
        bias_shard[: 2 * piece].reshape(2, piece),
        attn_shard[:, 3 * part :].T,
        out_bias_shard,
        feed_shard[:, :hid],
        up_bias_shard,
        feed_shard[:, hid:].T,
        down_bias_shard,
    )


def solution(mesh):
    in_specs = (
        P("fsdp", "ctx", None),
        P("fsdp", None),
        P(("fsdp", "ctx"), None, "tensor"),
        P(None, ("tensor", "fsdp", "ctx")),
        P(("fsdp", "ctx"), None, "tensor"),
        P(None, ("tensor", "fsdp", "ctx")),
        P("tensor", ("fsdp", "ctx")),
        P(("fsdp", "ctx")),
        P(("fsdp", "ctx"), "tensor"),
        P(("tensor", "fsdp", "ctx")),
        P("tensor", ("fsdp", "ctx")),
        P(("fsdp", "ctx")),
        P("fsdp", "ctx", None),
    )
    out_specs = (
        P("fsdp", "ctx", None),
        P("fsdp", "ctx", None),
        P("fsdp", None),
        P(("fsdp", "ctx"), None, "tensor"),
        P(None, ("tensor", "fsdp", "ctx")),
        P(("fsdp", "ctx"), None, "tensor"),
        P(None, ("tensor", "fsdp", "ctx")),
        P("tensor", ("fsdp", "ctx")),
        P(("fsdp", "ctx")),
        P(("fsdp", "ctx"), "tensor"),
        P(("tensor", "fsdp", "ctx")),
        P("tensor", ("fsdp", "ctx")),
        P(("fsdp", "ctx")),
    )
    return jax.shard_map(functools.partial(body, dict(mesh.shape)), mesh=mesh, in_specs=in_specs, out_specs=out_specs, check_vma=False)
```

```python
import functools
import math

import jax
import jax.numpy as jnp
from jax import lax
from jax.experimental import pallas as pl
from jax.experimental.pallas import tpu as pltpu
from jax.sharding import PartitionSpec as P

HEAD_DIM = 64


EPSILON = 1e-06
GELU_SCALE = 0.7978845608028654
GELU_CUBIC = 0.044715

PLANE = ("fsdp", "ctx")
EVERY = ("fsdp", "ctx", "tensor")


def layer_norm(values):
    center = values - jnp.mean(values, axis=-1, keepdims=True)
    spread = jnp.mean(center * center, axis=-1, keepdims=True)
    return center * lax.rsqrt(spread + EPSILON)


def gelu_tanh(pre_act):
    return (
        0.5
        * pre_act
        * (1.0 + jnp.tanh(GELU_SCALE * (pre_act + GELU_CUBIC * pre_act * pre_act * pre_act)))
    )


def silu_slope(values):
    sigmoid_val = jax.nn.sigmoid(values)
    return sigmoid_val * (1.0 + values * (1.0 - sigmoid_val))


def total_of(sizes, axes):
    return math.prod(sizes[a] for a in axes)


def index_of(sizes, axes):
    me = 0
    for a in axes:
        me = me * sizes[a] + lax.axis_index(a)
    return me


def coords_of(sizes, axes, index):
    found = {}
    for a in reversed(axes):
        found[a] = lax.rem(index, sizes[a])
        index = lax.div(index, sizes[a])
    return {a: found[a] for a in axes}


def exchange_kernel(sizes, groups, *refs):
    count = sum(len(cuts) for _, cuts in groups)
    ins, outs = refs[:count], refs[count : 2 * count]
    sems = refs[2 * count :]
    barrier = pltpu.get_barrier_semaphore()

    def neighbours(axes):
        n = total_of(sizes, axes)
        me = index_of(sizes, axes)

        def peer_of(step):
            return lax.rem(me + step, n)

        return n, me, peer_of

    for axes, _ in groups:
        n, me, peer_of = neighbours(axes)

        def greet(step, carry, axes=axes, peer_of=peer_of):
            pl.semaphore_signal(
                barrier,
                inc=1,
                device_id=coords_of(sizes, axes, peer_of(step)),
                device_id_type=pl.DeviceIdType.MESH,
            )
            return carry

        lax.fori_loop(1, n, greet, 0)
    pl.semaphore_wait(barrier, sum(total_of(sizes, axes) - 1 for axes, _ in groups))

    pending = []
    own = []
    first = 0
    for place, (axes, cuts) in enumerate(groups):
        n, me, peer_of = neighbours(axes)
        send_sem, recv_sem, own_sem = sems[3 * place : 3 * place + 3]

        def copies(step, axes=axes, cuts=cuts, first=first, me=me, peer_of=peer_of, sends=send_sem, recvs=recv_sem):
            peer = peer_of(step)
            return [
                pltpu.make_async_remote_copy(
                    src_ref=cut_in(ins[first + i], peer),
                    dst_ref=cut_out(outs[first + i], me),
                    send_sem=sends.at[i, step - 1],
                    recv_sem=recvs.at[i, step - 1],
                    device_id=coords_of(sizes, axes, peer),
                    device_id_type=pl.DeviceIdType.MESH,
                )
                for i, (cut_in, cut_out) in enumerate(cuts)
            ]

        def begin(step, carry, copies=copies):
            for copy in copies(step):
                copy.start()
            return carry

        def finish(step, carry, copies=copies):
            for copy in copies(step):
                copy.wait()
            return carry

        lax.fori_loop(1, n, begin, 0)
        pending.append((n, finish))
        own += [
            pltpu.make_async_copy(
                cut_in(ins[first + i], me), cut_out(outs[first + i], me), own_sem.at[i]
            )
            for i, (cut_in, cut_out) in enumerate(cuts)
        ]
        first += len(cuts)
    for copy in own:
        copy.start()
    for copy in own:
        copy.wait()
    for n, finish in pending:
        lax.fori_loop(1, n, finish, 0)


def whole_ref(ref, index):
    return ref


def lead(ref, index):
    return ref.at[index]


def rows(width):
    def cut(ref, index):
        return ref.at[:, pl.ds(pl.multiple_of(index * width, width), width), :]

    return cut


def exchange(sizes, axes, collective_id, items, more=()):
    groups = [(axes, items)] + list(more)
    every = [item for _, members in groups for item in members]
    scratch = []
    for near, members in groups:
        pairs = pltpu.SemaphoreType.DMA((len(members), total_of(sizes, near) - 1))
        scratch += [pairs, pairs, pltpu.SemaphoreType.DMA((len(members),))]
    return pl.pallas_call(
        functools.partial(
            exchange_kernel,
            sizes,
            [(near, [(item[1], item[2]) for item in members]) for near, members in groups],
        ),
        out_shape=[jax.ShapeDtypeStruct(item[3], item[0].dtype) for item in every],
        in_specs=[pl.BlockSpec(memory_space=pl.ANY)] * len(every),
        out_specs=[pl.BlockSpec(memory_space=pl.ANY)] * len(every),
        scratch_shapes=scratch,
        compiler_params=pltpu.CompilerParams(
            collective_id=collective_id, has_side_effects=True
        ),
    )(*[item[0] for item in every])


def gather_item(x, n):
    return (x, whole_ref, lead, (n,) + x.shape)


def scatter_item(x):
    return (x, lead, lead, x.shape)


def gather_rows_item(x, n):
    return (x, whole_ref, rows(x.shape[1]), (x.shape[0], n * x.shape[1], x.shape[2]))


def scatter_rows_item(x, n):
    width = x.shape[1] // n
    return (x, rows(width), lead, (n, x.shape[0], width, x.shape[2]))


def relay_kernel(sizes, x_ref, out_ref, near_send, near_recv, far_send, far_recv, pass_send, pass_recv, own_sem):
    n = sizes["ctx"]
    half = n // 2
    blocks, width = x_ref.shape[0], x_ref.shape[1]
    me = lax.axis_index("ctx")
    mate = me + 1 - 2 * lax.rem(me, 2)

    def peer(step):
        return lax.rem(me + 2 * step, n)

    def source(step):
        return lax.rem(me + n - 2 * step, n)

    def place(block, index):
        return out_ref.at[block, pl.ds(pl.multiple_of(index * width, width), width), :]

    barrier = pltpu.get_barrier_semaphore()
    for other in [mate] + [peer(step) for step in range(1, half)]:
        pl.semaphore_signal(
            barrier, inc=1, device_id={"ctx": other}, device_id_type=pl.DeviceIdType.MESH
        )
    pl.semaphore_wait(barrier, half)

    def remote(src, dst, send, recv, other):
        return pltpu.make_async_remote_copy(
            src_ref=src,
            dst_ref=dst,
            send_sem=send,
            recv_sem=recv,
            device_id={"ctx": other},
            device_id_type=pl.DeviceIdType.MESH,
        )

    far = {}
    for block in range(blocks):
        for step in range(1, half):
            far[block, step] = remote(
                x_ref.at[block],
                place(block, me),
                far_send.at[block, step - 1],
                far_recv.at[block, step - 1],
                peer(step),
            )
            far[block, step].start()
    near = []
    for block in range(blocks):
        near.append(
            remote(x_ref.at[block], place(block, me), near_send.at[block], near_recv.at[block], mate)
        )
        near[-1].start()
    own = [
        pltpu.make_async_copy(x_ref.at[block], place(block, me), own_sem.at[block])
        for block in range(blocks)
    ]
    for copy in own:
        copy.start()
    passed = []
    for block in range(blocks):
        for step in range(1, half):
            far[block, step].wait_recv()
            landed = place(block, source(step))
            passed.append(
                remote(
                    landed,
                    landed,
                    pass_send.at[block, step - 1],
                    pass_recv.at[block, step - 1],
                    mate,
                )
            )
            passed[-1].start()
    for copy in far.values():
        copy.wait_send()
    for copy in own:
        copy.wait()
    for copy in near + passed:
        copy.wait()


def relay_gather(sizes, collective_id, x):
    n = sizes["ctx"]
    blocks = x.shape[0]
    cross = pltpu.SemaphoreType.DMA((blocks, n // 2 - 1))
    near = pltpu.SemaphoreType.DMA((blocks,))
    return pl.pallas_call(
        functools.partial(relay_kernel, sizes),
        out_shape=jax.ShapeDtypeStruct((blocks, n * x.shape[1], x.shape[2]), x.dtype),
        in_specs=[pl.BlockSpec(memory_space=pl.ANY)],
        out_specs=pl.BlockSpec(memory_space=pl.ANY),
        scratch_shapes=[near, near, cross, cross, cross, cross, near],
        compiler_params=pltpu.CompilerParams(
            collective_id=collective_id, has_side_effects=True
        ),
    )(x)


def body(
    sizes,
    latents_in,
    conditioning,
    ada_weight,
    ada_bias,
    qkv_weight,
    qv_bias,
    out_weight,
    out_bias,
    up_weight,
    up_bias,
    down_weight,
    down_bias,
    cotangent,
):
    f32, bf16 = jnp.float32, jnp.bfloat16
    n_fsdp, n_ctx, n_tensor = sizes["fsdp"], sizes["ctx"], sizes["tensor"]
    n_plane = n_fsdp * n_ctx
    plane_me = index_of(sizes, PLANE)
    fsdp_me = lax.axis_index("fsdp")
    tensor_me = lax.axis_index("tensor")
    latent_count, tok_rows, width = latents_in.shape
    own_rows = tok_rows // n_tensor
    depth = qkv_weight.shape[0]
    part = qkv_weight.shape[2]
    hid = up_weight.shape[1]
    local_heads = part // HEAD_DIM
    score_scale = 1.0 / math.sqrt(HEAD_DIM)

    def own(x):
        return lax.dynamic_slice_in_dim(x, tensor_me * own_rows, own_rows, 1)

    qkv_full = lax.all_gather(qkv_weight.reshape(depth, 3 * part), PLANE, axis=0, tiled=True)
    late_weights = jnp.concatenate([up_weight, down_weight.T], axis=1)
    late_weights, _ = lax.optimization_barrier((late_weights, qkv_full))
    late_full = lax.all_gather(late_weights, PLANE, axis=0, tiled=True)
    out_all = lax.all_gather(out_weight.T, ("tensor",) + PLANE, axis=0)
    out_back = (
        out_all.reshape(n_tensor, width, part).transpose(1, 0, 2).reshape(width, width)
    )

    cond = conditioning.astype(f32)
    biases = jnp.concatenate(
        [ada_bias.reshape(-1), qv_bias.reshape(-1), out_bias, up_bias, down_bias]
    )
    bias_len = biases.shape[0]
    bias_pad = -bias_len % 128
    biases = jnp.pad(biases.astype(f32), (0, bias_pad)).reshape(-1, 128)
    cond_all, bias_all = exchange(
        sizes,
        PLANE,
        1,
        [
            gather_item(cond, n_plane),
            gather_item(biases, n_plane),
        ],
    )
    bias_all = bias_all.reshape(n_plane, -1)
    piece = part // n_plane
    six = ada_bias.shape[0]
    at = 0
    ada_shift = bias_all[:, at : at + six * piece].reshape(n_plane, six, piece)
    ada_shift = ada_shift.transpose(1, 0, 2).reshape(six, part)
    at += six * piece
    qv_shift = bias_all[:, at : at + 2 * piece].reshape(n_plane, 2, piece)
    qv_shift = qv_shift.transpose(1, 0, 2).reshape(2, part)
    at += 2 * piece
    out_shift = bias_all[:, at : at + depth].reshape(width)
    at += depth
    up_piece = up_bias.shape[0]
    up_shift = bias_all[:, at : at + up_piece].reshape(hid)
    at += up_piece
    down_shift = bias_all[:, at : at + depth].reshape(width)

    cond_every = cond_all.reshape(n_fsdp, n_ctx, latent_count, width)[:, 0]
    cond_every = cond_every.reshape(n_fsdp * latent_count, width)
    cond_mine = lax.dynamic_slice_in_dim(cond_every, plane_me * depth, depth, 1)
    lifted_mine = jax.nn.silu(cond_mine).astype(bf16)
    ada_flat = ada_weight.reshape(depth, six * part)
    mod_terms = jnp.dot(lifted_mine, ada_flat, preferred_element_type=f32)
    mod_terms = mod_terms.reshape(n_fsdp, latent_count, six * part)

    def by_fsdp(ref, index):
        return ref.at[lax.div(index, n_ctx)]

    (mod_pieces,) = exchange(
        sizes,
        PLANE,
        2,
        [(mod_terms, by_fsdp, lead, (n_plane, latent_count, six * part))],
    )
    mod_part = jnp.sum(mod_pieces, axis=0) + ada_shift.reshape(1, six * part)
    (mod_all,) = exchange(sizes, ("tensor",), 3, [gather_item(mod_part, n_tensor)])
    modulation = (
        mod_all.reshape(n_tensor, latent_count, six, part)
        .transpose(1, 2, 0, 3)
        .reshape(latent_count, six, width)
    )
    shift_one, scale_one, gate_one, shift_two, scale_two, gate_two = [
        modulation[:, offset][:, None, :] for offset in range(6)
    ]

    inputs = latents_in.astype(f32)
    shifted = (layer_norm(inputs) * (1.0 + scale_one) + shift_one).astype(bf16)
    inputs_own = own(latents_in).astype(f32)
    normed_own, norm_back = jax.vjp(layer_norm, inputs_own)

    project = jnp.einsum("bld,de->ble", shifted, qkv_full, preferred_element_type=f32)
    queries = (project[:, :, :part] + qv_shift[0]).astype(bf16)
    keys_values = jnp.concatenate(
        [project[:, :, part : 2 * part], project[:, :, 2 * part :] + qv_shift[1]], axis=2
    ).astype(bf16)
    kv_all = relay_gather(sizes, 4, keys_values)
    seq_len = kv_all.shape[1]
    query_heads = queries.reshape(latent_count, tok_rows, local_heads, HEAD_DIM)
    key_heads = kv_all[:, :, :part].reshape(latent_count, seq_len, local_heads, HEAD_DIM)
    value_heads = kv_all[:, :, part:].reshape(latent_count, seq_len, local_heads, HEAD_DIM)
    scores = (
        jnp.einsum("bqhe,bkhe->bhqk", query_heads, key_heads, preferred_element_type=f32)
        * score_scale
    )
    log_total = jax.nn.logsumexp(scores, axis=-1, keepdims=True)
    prob_low = jnp.exp(scores - log_total).astype(bf16)
    mixed_heads = (
        jnp.einsum("bhqk,bkhe->bqhe", prob_low, value_heads, preferred_element_type=f32)
        .astype(bf16)
        .reshape(latent_count, tok_rows, part)
    )
    up_full = late_full[:, :hid]
    down_back = late_full[:, hid:]
    (mixed_pieces,) = exchange(
        sizes, ("tensor",), 5, [scatter_rows_item(mixed_heads, n_tensor)]
    )
    mixed_own = jnp.concatenate([mixed_pieces[z] for z in range(n_tensor)], axis=2)
    attended = (
        jnp.einsum("bld,ed->ble", mixed_own, out_back, preferred_element_type=f32) + out_shift
    )
    after_attn = inputs_own + gate_one * attended
    normed_two, norm_back_two = jax.vjp(layer_norm, after_attn)
    shifted_two_own = (normed_two * (1.0 + scale_two) + shift_two).astype(bf16)
    (shifted_two,) = exchange(
        sizes, ("tensor",), 6, [gather_rows_item(shifted_two_own, n_tensor)]
    )
    hidden_pre = (
        jnp.einsum("bld,df->blf", shifted_two, up_full, preferred_element_type=f32) + up_shift
    )
    hidden_val, gelu_back = jax.vjp(gelu_tanh, hidden_pre)
    hidden = hidden_val.astype(bf16)
    feed_part = jnp.einsum("blf,df->bld", hidden, down_back, preferred_element_type=f32)
    feed_sum = lax.psum_scatter(
        feed_part.astype(bf16), "tensor", scatter_dimension=1, tiled=True
    )
    feed_out = feed_sum.astype(f32) + down_shift
    block_own = (after_attn + gate_two * feed_out).astype(bf16)

    upstream_own = own(cotangent).astype(f32)
    feed_grad = (gate_two * cotangent.astype(f32)).astype(bf16)
    gate_two_grad = jnp.sum(upstream_own * feed_out, axis=1)
    down_bias_grad = jnp.sum(feed_grad.astype(f32), axis=(0, 1))
    hidden_grad = jnp.einsum("bld,df->blf", feed_grad, down_back, preferred_element_type=f32)
    pre_grad = gelu_back(hidden_grad)[0].astype(bf16)
    two_part = jnp.einsum("blf,df->bld", pre_grad, up_full, preferred_element_type=f32)
    (two_pieces,) = exchange(
        sizes, ("tensor",), 7, [scatter_rows_item(two_part.astype(bf16), n_tensor)]
    )
    up_bias_grad = jnp.sum(pre_grad.astype(f32), axis=(0, 1))
    up_weight_grad = jnp.einsum(
        "bld,blf->df", shifted_two, pre_grad, preferred_element_type=f32
    )
    down_weight_grad = jnp.einsum("bld,blf->df", feed_grad, hidden, preferred_element_type=f32)
    feed_weights = jnp.concatenate(
        [up_weight_grad.astype(bf16), down_weight_grad.astype(bf16)], axis=1
    )
    feed_shard = lax.psum_scatter(feed_weights, PLANE, scatter_dimension=0, tiled=True)
    feed_shard = feed_shard.astype(f32)

    shifted_two_grad = jnp.sum(two_pieces.astype(f32), axis=0)
    scale_two_grad = jnp.sum(shifted_two_grad * normed_two, axis=1)
    shift_two_grad = jnp.sum(shifted_two_grad, axis=1)
    after_grad = upstream_own + norm_back_two(shifted_two_grad * (1.0 + scale_two))[0]
    attn_grad_own = (gate_one * after_grad).astype(bf16)
    gate_one_grad = jnp.sum(after_grad * attended, axis=1)
    mixed_grad_own = jnp.einsum(
        "ble,ed->bld", attn_grad_own, out_back, preferred_element_type=f32
    ).astype(bf16)
    mixed_grad_cut = jnp.stack(
        [mixed_grad_own[:, :, z * part : (z + 1) * part] for z in range(n_tensor)]
    )
    mixed_grad_cut, block_own = lax.optimization_barrier((mixed_grad_cut, block_own))
    (mixed_grad,) = exchange(
        sizes,
        ("tensor",),
        8,
        [(mixed_grad_cut, lead, rows(own_rows), (latent_count, tok_rows, part))],
    )
    block_out = lax.all_gather(block_own, "tensor", axis=1, tiled=True)
    out_bias_part = jnp.sum(attn_grad_own.astype(f32), axis=(0, 1))
    out_weight_part = jnp.einsum(
        "zbld,ble->zde", mixed_pieces, attn_grad_own, preferred_element_type=f32
    ).astype(bf16)
    out_weight_grad = lax.psum_scatter(
        out_weight_part.reshape(width, width), "tensor", scatter_dimension=0, tiled=True
    ).T
    mixed_grad = mixed_grad.reshape(latent_count, tok_rows, local_heads, HEAD_DIM)
    scores_again = (
        jnp.einsum("bqhe,bkhe->bhqk", query_heads, key_heads, preferred_element_type=f32)
        * score_scale
    )
    probs = jnp.exp(scores_again - log_total)
    prob_grad = jnp.einsum("bqhe,bkhe->bhqk", mixed_grad, value_heads, preferred_element_type=f32)
    row_term = jnp.sum(probs * prob_grad, axis=-1, keepdims=True)
    score_grad = (probs * (prob_grad - row_term)).astype(bf16)
    query_grad = (
        jnp.einsum("bhqk,bkhe->bqhe", score_grad, key_heads, preferred_element_type=f32)
        * score_scale
    ).astype(bf16)
    query_grad = query_grad.reshape(latent_count, tok_rows, part)
    probs_again = probs.astype(bf16)
    key_term = (
        jnp.einsum("bhqk,bqhe->bkhe", score_grad, query_heads, preferred_element_type=f32)
        * score_scale
    ).reshape(latent_count, seq_len, part)
    value_term = jnp.einsum(
        "bhqk,bqhe->bkhe", probs_again, mixed_grad, preferred_element_type=f32
    ).reshape(latent_count, seq_len, part)
    kv_term = jnp.concatenate([key_term.astype(bf16), value_term.astype(bf16)], axis=2)
    (kv_pieces,) = exchange(sizes, ("ctx",), 9, [scatter_rows_item(kv_term, n_ctx)])
    kv_grad = jnp.sum(kv_pieces.astype(f32), axis=0).astype(bf16)
    proj_grad = jnp.concatenate([query_grad, kv_grad], axis=2)
    proj_bias_grad = jnp.sum(proj_grad.astype(f32), axis=(0, 1)).reshape(3, part)
    one_part = jnp.einsum("ble,de->bld", proj_grad, qkv_full, preferred_element_type=f32)
    one_low, block_out = lax.optimization_barrier((one_part.astype(bf16), block_out))
    (one_pieces,) = exchange(
        sizes, ("tensor",), 10, [scatter_rows_item(one_low, n_tensor)]
    )
    qkv_weight_grad = jnp.einsum("bld,ble->de", shifted, proj_grad, preferred_element_type=f32)

    shifted_grad = jnp.sum(one_pieces.astype(f32), axis=0)
    scale_one_grad = jnp.sum(shifted_grad * normed_own, axis=1)
    shift_one_grad = jnp.sum(shifted_grad, axis=1)
    grad_in_own = after_grad + norm_back(shifted_grad * (1.0 + scale_one))[0]
    mod_grad_own = jnp.stack(
        [
            shift_one_grad,
            scale_one_grad,
            gate_one_grad,
            shift_two_grad,
            scale_two_grad,
            gate_two_grad,
        ],
        axis=1,
    )
    mod_grad_own = (
        mod_grad_own.reshape(latent_count, six, n_tensor, part)
        .transpose(2, 0, 1, 3)
        .reshape(n_tensor, latent_count, six * part)
    )
    bias_grads = jnp.concatenate(
        [
            proj_bias_grad[0].reshape(n_plane, piece),
            proj_bias_grad[2].reshape(n_plane, piece),
            up_bias_grad.reshape(n_plane, up_piece),
            down_bias_grad.reshape(n_plane, depth),
        ],
        axis=1,
    )
    bias_grads = jnp.pad(bias_grads, ((0, 0), (0, -bias_grads.shape[1] % 128)))
    bias_grads = bias_grads.reshape(n_plane, -1, 128)
    attn_weights = jnp.concatenate(
        [qkv_weight_grad.astype(bf16), out_weight_grad.astype(bf16)], axis=1
    ).reshape(n_plane, depth, 4 * part)
    mod_pieces_back, out_bias_pieces, weight_pieces, bias_pieces = exchange(
        sizes,
        ("tensor",),
        11,
        [scatter_item(mod_grad_own), gather_item(out_bias_part.reshape(-1, 128), n_tensor)],
        [(PLANE, [scatter_item(attn_weights), scatter_item(bias_grads)])],
    )
    grad_in_low = grad_in_own.astype(bf16)
    grad_in_all = lax.all_gather(grad_in_low, "tensor", axis=1, tiled=True)
    mod_grad_part = jnp.sum(mod_pieces_back, axis=0)
    out_bias_grad = jnp.sum(out_bias_pieces, axis=0).reshape(n_plane, depth)
    mod_every, out_bias_every = exchange(
        sizes,
        PLANE,
        12,
        [
            gather_item(mod_grad_part, n_plane),
            scatter_item(out_bias_grad.reshape(n_plane, 1, depth)),
        ],
    )
    attn_shard = jnp.sum(weight_pieces.astype(f32), axis=0)
    bias_shard = jnp.sum(bias_pieces, axis=0).reshape(-1)
    mod_grad = jnp.sum(
        mod_every.reshape(n_fsdp, n_ctx, latent_count, six * part), axis=1
    ).astype(bf16)
    mod_grad = mod_grad.reshape(n_fsdp * latent_count, six * part)
    ada_weight_grad = jnp.einsum(
        "bd,be->de", lifted_mine, mod_grad, preferred_element_type=f32
    ).reshape(depth, six, part)
    ada_bias_sum = jnp.sum(mod_grad.astype(f32), axis=0).reshape(six, part)
    ada_bias_grad = lax.dynamic_slice_in_dim(ada_bias_sum, plane_me * piece, piece, 1)
    lifted_part = jnp.einsum("be,de->bd", mod_grad, ada_flat, preferred_element_type=f32)
    lifted_part, grad_in_all = lax.optimization_barrier((lifted_part, grad_in_all))
    grad_in = grad_in_all.astype(f32)
    (lifted_all,) = exchange(
        sizes, EVERY, 13, [gather_item(lifted_part, n_plane * n_tensor)]
    )
    lifted_grad = jnp.sum(
        lifted_all.reshape(n_plane, n_tensor, n_fsdp, latent_count, depth), axis=1
    )
    lifted_grad = lax.dynamic_index_in_dim(lifted_grad, fsdp_me, 1, keepdims=False)
    lifted_grad = lifted_grad.transpose(1, 0, 2).reshape(latent_count, width)
    grad_cond = lifted_grad * silu_slope(cond)

    at = 2 * piece
    out_bias_shard = jnp.sum(out_bias_every, axis=0).reshape(depth)
    up_bias_shard = bias_shard[at : at + up_piece]
    at += up_piece
    down_bias_shard = bias_shard[at : at + depth]
    return (
        block_out,
        grad_in,
        grad_cond,
        ada_weight_grad,
        ada_bias_grad,
        attn_shard[:, : 3 * part].reshape(depth, 3, part),
        bias_shard[: 2 * piece].reshape(2, piece),
        attn_shard[:, 3 * part :].T,
        out_bias_shard,
        feed_shard[:, :hid],
        up_bias_shard,
        feed_shard[:, hid:].T,
        down_bias_shard,
    )


def solution(mesh):
    in_specs = (
        P("fsdp", "ctx", None),
        P("fsdp", None),
        P(("fsdp", "ctx"), None, "tensor"),
        P(None, ("tensor", "fsdp", "ctx")),
        P(("fsdp", "ctx"), None, "tensor"),
        P(None, ("tensor", "fsdp", "ctx")),
        P("tensor", ("fsdp", "ctx")),
        P(("fsdp", "ctx")),
        P(("fsdp", "ctx"), "tensor"),
        P(("tensor", "fsdp", "ctx")),
        P("tensor", ("fsdp", "ctx")),
        P(("fsdp", "ctx")),
        P("fsdp", "ctx", None),
    )
    out_specs = (
        P("fsdp", "ctx", None),
        P("fsdp", "ctx", None),
        P("fsdp", None),
        P(("fsdp", "ctx"), None, "tensor"),
        P(None, ("tensor", "fsdp", "ctx")),
        P(("fsdp", "ctx"), None, "tensor"),
        P(None, ("tensor", "fsdp", "ctx")),
        P("tensor", ("fsdp", "ctx")),
        P(("fsdp", "ctx")),
        P(("fsdp", "ctx"), "tensor"),
        P(("tensor", "fsdp", "ctx")),
        P("tensor", ("fsdp", "ctx")),
        P(("fsdp", "ctx")),
    )
    return jax.shard_map(functools.partial(body, dict(mesh.shape)), mesh=mesh, in_specs=in_specs, out_specs=out_specs, check_vma=False)
```
